32 devices in a mesh: req: 8 (over z, y), head: 4 (over x, core).
Axes of the slice: x: 2, y: 2, z: 4, core: 2. Of those that a mesh axis runs over, the one named last changes fastest.
Arguments:
- tokens: bfloat16 [512, 1024], P(('req', 'head')), may hold values from -6 to 6
- gains: float32 [2, 1024], replicated, may hold values from 0.1 to 1.9
- qkv_weight: bfloat16 [3, 1024, 1024], P(None, None, 'head'), may hold values from -0.1875 to 0.1875
- out_weight: bfloat16 [1024, 1024], replicated, may hold values from -0.1875 to 0.1875
- gate_up_weight: bfloat16 [2, 1024, 4096], P(None, None, 'head'), may hold values from -0.1875 to 0.1875
- down_weight: bfloat16 [4096, 1024], P('head'), may hold values from -0.09375 to 0.09375
- variate_bias: float32 [2, 16], replicated, may hold values from -4 to 4
- page_cache: bfloat16 [2, 160, 128, 1024], P(None, 'req', None, 'head'), may hold values from -210 to 210
- page_variates: int32 [160, 128], P('req'), may hold values from 0 to 3
- token_variates: int32 [512], replicated, may hold values from 0 to 3
- cache_len: int32 [8], replicated, may hold values from 64 to 4096, as said below
- page_table: int32 [8, 32], replicated, may hold values from -1 to 159, as said below
- parents: int32 [8, 64], P('req'), may hold values from -1 to 55, as said below
- accepted: int32 [8, 8], P('req'), may hold values from -1 to 63, as said below
Outputs:
- mixed: bfloat16 [512, 1024], P(('req', 'head'))
- attended: bfloat16 [512, 1024], P('req', 'head')
- new_kv: bfloat16 [2, 8, 8, 1024], P(None, 'req', None, 'head')
The draws below stay inside these ranges and needn't reach their ends.
Inputs may be any that keep to these rules, and one draw needn't show every extreme that they name: `cache_len`: exactly half of the requests have 128 // 2 to 128 cached positions, the others 4096 // 2 + 1 to 4096. `page_table`: entry [r, b] is the page holding request r's positions b * 128 to b * 128 + 127 for b below ceil(cache_len[r] / 128), and -1 from there on; no page is listed twice. `parents`: node i lies on level i // 8; nodes of level 0 have parent -1, every other node's parent lies on the level before. `accepted`: row r lists a path of request r's tree from a level-0 node downward, one node a level, then -1; its length is 1 to 8, and 8 in some row.
All inputs are finite; a program needn't handle non-finite values.
Results may differ from the reference program's by a relative error of at most 0.015.
The reference program's roundings to bfloat16 on the way (of `normed`, `weights`, `hidden_state`, `normed_two` and `activated`) count: a program that leaves them out, or rounds other values in their place, can miss the bound.
Values may be sent and summed in bfloat16 or wider, within the bound.
A program may use at most 192 MiB of HBM per device.

```python
import math
import jax
import jax.numpy as jnp
from jax import lax

D = 1024
HEADS = 16
HD = 64
FF = 4096
BRANCH = 8
LEVELS = 8
PAGE = 128
MAXP = 32
NVAR = 4
TREE = 64
QD = 1024
CACHE = 4096
REQUESTS = 8
TOKENS = 512
PAGES = 160


def lengths_and_table(key):
    base = jax.random.fold_in(key, 11)
    key_order, key_short, key_long, key_pages = jax.random.split(base, 4)
    order = jax.random.permutation(key_order, REQUESTS)
    short_len = jax.random.randint(key_short, (REQUESTS,), PAGE // 2, PAGE + 1)
    long_len = jax.random.randint(key_long, (REQUESTS,), CACHE // 2 + 1, CACHE + 1)
    lengths = jnp.where(order < REQUESTS // 2, long_len, short_len)
    lengths = jnp.where(order == 0, CACHE, lengths)
    lengths = jnp.where(order == REQUESTS - 1, PAGE // 2, lengths)
    counts = (lengths + PAGE - 1) // PAGE
    offsets = jnp.cumsum(counts) - counts
    shuffled = jax.random.permutation(key_pages, PAGES).astype(jnp.int32)
    first_page = shuffled[0]
    place = jnp.arange(PAGES, dtype=jnp.int32)
    shuffled = jnp.where(place == 0, PAGES - 1, jnp.where(shuffled == PAGES - 1, first_page, shuffled))
    column = jnp.arange(MAXP, dtype=jnp.int32)
    index = jnp.clip(offsets[:, None] + column[None, :], 0, PAGES - 1)
    table = jnp.where(column[None, :] < counts[:, None], shuffled[index], -1)
    return (lengths.astype(jnp.int32), table.astype(jnp.int32))


def draw_cache_len(key, part):
    return lengths_and_table(key)[0]


def draw_page_table(key, part):
    return lengths_and_table(key)[1]


def tree_and_path(key):
    base = jax.random.fold_in(key, 23)
    key_pick, key_depth, key_forced, key_leaf = jax.random.split(base, 4)
    nodes = jnp.arange(TREE, dtype=jnp.int32)
    level = nodes // BRANCH
    pick = jax.random.randint(key_pick, (REQUESTS, TREE), 0, BRANCH)
    request_ids = jnp.arange(REQUESTS, dtype=jnp.int32)
    pick = jnp.where((request_ids[:, None] == 0) & (nodes[None, :] == TREE - 1), BRANCH - 1, pick)
    parent_rows = jnp.where(level[None, :] >= 1, (level[None, :] - 1) * BRANCH + pick, -1)
    depth = jax.random.randint(key_depth, (REQUESTS,), 1, LEVELS + 1)
    forced = jax.random.randint(key_forced, (), 0, REQUESTS)
    shallow = (forced + 1) % REQUESTS
    depth = jnp.where(request_ids == shallow, 1, depth)
    depth = jnp.where(request_ids == forced, LEVELS, depth)
    leaf = jax.random.randint(key_leaf, (REQUESTS,), 0, BRANCH)
    leaf = jnp.where(request_ids == forced, BRANCH - 1, leaf)
    current = (depth - 1) * BRANCH + leaf
    upward = []
    for step in range(LEVELS):
        upward.append(current)
        above = jnp.take_along_axis(parent_rows, jnp.maximum(current, 0)[:, None], axis=1)[:, 0]
        current = jnp.where(current >= 0, above, -1)
    climb = jnp.stack(upward, axis=1)
    column = jnp.arange(LEVELS, dtype=jnp.int32)
    source = depth[:, None] - 1 - column[None, :]
    path = jnp.where(source >= 0, jnp.take_along_axis(climb, jnp.maximum(source, 0), axis=1), -1)
    return (parent_rows.astype(jnp.int32), path.astype(jnp.int32))


def draw_parents(key, part):
    return tree_and_path(key)[0]


def draw_accepted(key, part):
    return tree_and_path(key)[1]


def draw_page_cache(key, part):
    key_base = jax.random.fold_in(key, 0)
    shape = (2, PAGES, PAGE, QD)
    result = jnp.clip(jax.random.normal(key_base, shape, jnp.float32) * 2.0, -12.0, 12.0)
    return result.astype(jnp.bfloat16)


def touch_ends(values, key, low, top_value):
    extent = values.shape
    spot = [jax.random.randint(jax.random.fold_in(key, axis), (), 0, extent[axis]) for axis in range(len(extent))]
    values = values.at[tuple(spot)].set(low)
    longest = extent.index(max(extent))
    spot[longest] = (spot[longest] + 1) % extent[longest]
    return values.at[tuple(spot)].set(top_value)


def levels(stream_key, dims, shards, low, largest):
    factor_of, own = 1.0, jax.random.fold_in(stream_key, 6)
    for dim, shards_of in shards:
        steps = jnp.exp(jax.random.uniform(jax.random.fold_in(own, dim), (shards_of,), jnp.float32, low / len(shards), largest / len(shards)))
        factor_of = factor_of * jnp.repeat(steps, dims[dim] // shards_of).reshape([-1 if axis == dim else 1 for axis in range(len(dims))])
    return factor_of


def scatter_about(stream_key, shape, scale, most, cuts=(), held_as=jnp.bfloat16):
    array = jax.random.normal(stream_key, shape, jnp.float32) * scale
    if len(cuts) > 0:
        array = levels(stream_key, shape, cuts, -0.22, 0.18) * array
    return jnp.clip(array, min=-most, max=most).astype(held_as)


def setup_inputs(seed: int = 0) -> dict:
    arg_keys = jax.random.split(jax.random.key(seed), 15)
    tokens = scatter_about(arg_keys[0], (TOKENS, D), 1.0, 6.0, ((0, 32),))
    gains = jnp.clip(1.0 + 0.18 * jax.random.normal(arg_keys[1], (2, D), jnp.float32), 0.1, 1.9)
    qkv_weight = scatter_about(arg_keys[2], (3, D, QD), D ** -0.5, 0.1875, ((2, 4),))
    out_weight = scatter_about(arg_keys[3], (QD, D), QD ** -0.5, 0.1875)
    gate_up_weight = scatter_about(arg_keys[4], (2, D, FF), D ** -0.5, 0.1875, ((2, 4),))
    down_weight = scatter_about(arg_keys[5], (FF, D), FF ** -0.5, 0.09375, ((0, 4),))
    variate_bias = scatter_about(arg_keys[6], (2, HEADS), 1.0, 4.0, (), jnp.float32)
    page_cache = draw_page_cache(jax.random.fold_in(arg_keys[14], 71), 0)
    page_variates = touch_ends(jax.random.randint(arg_keys[8], (PAGES, PAGE), 0, NVAR), jax.random.fold_in(arg_keys[8], 1), 0, NVAR - 1).astype(jnp.int32)
    token_variates = touch_ends(jax.random.randint(arg_keys[9], (TOKENS,), 0, NVAR), jax.random.fold_in(arg_keys[9], 1), 0, NVAR - 1).astype(jnp.int32)
    cache_len = draw_cache_len(jax.random.fold_in(arg_keys[14], 71), 0)
    page_table = draw_page_table(jax.random.fold_in(arg_keys[14], 71), 0)
    parents = draw_parents(jax.random.fold_in(arg_keys[14], 71), 0)
    accepted = draw_accepted(jax.random.fold_in(arg_keys[14], 71), 0)
    return dict(tokens=tokens, gains=gains, qkv_weight=qkv_weight, out_weight=out_weight, gate_up_weight=gate_up_weight, down_weight=down_weight, variate_bias=variate_bias, page_cache=page_cache, page_variates=page_variates, token_variates=token_variates, cache_len=cache_len, page_table=page_table, parents=parents, accepted=accepted)


epsilon = 1e-06
masked_score = -1e+30
highest = lax.Precision.HIGHEST

def rms_scaled(rows, gain):
    values = rows.astype(jnp.float32)
    return values * lax.rsqrt(lax.optimization_barrier(jnp.mean(values * values, axis=-1, keepdims=True)) + epsilon) * gain

def ancestry(parent_row):
    width = parent_row.shape[0]
    nodes = jnp.arange(width, dtype=jnp.int32)
    reach = (parent_row[:, None] == nodes[None, :]).astype(jnp.float32) + jnp.eye(width, dtype=jnp.float32)
    for step in range(LEVELS.bit_length()):
        reach = jnp.minimum(jnp.dot(reach, reach, precision=highest), 1.0)
    return reach > 0.5

def reference(tokens, gains, qkv_weight, out_weight, gate_up_weight, down_weight, variate_bias, page_cache, page_variates, token_variates, cache_len, page_table, parents, accepted):
    scale = 1.0 / math.sqrt(HD)
    normed = rms_scaled(tokens, gains[0]).astype(jnp.bfloat16)
    query = jnp.dot(normed, qkv_weight[0], preferred_element_type=jnp.float32).astype(jnp.bfloat16)
    key_rows = jnp.dot(normed, qkv_weight[1], preferred_element_type=jnp.float32).astype(jnp.bfloat16)
    value_rows = jnp.dot(normed, qkv_weight[2], preferred_element_type=jnp.float32).astype(jnp.bfloat16)
    same_bias = variate_bias[0]
    other_bias = variate_bias[1]

    def one_request(inputs):
        request_query, request_key, request_value, table, length, parent_row, variates = inputs
        slots = jnp.where(table >= 0, table, 0)
        page_keys = jnp.take(page_cache[0], slots, axis=0).reshape(MAXP, PAGE, HEADS, HD).astype(jnp.float32)
        page_values = jnp.take(page_cache[1], slots, axis=0).reshape(MAXP, PAGE, HEADS, HD).astype(jnp.float32)
        cached_variates = jnp.take(page_variates, slots, axis=0)
        positions = jnp.arange(MAXP)[:, None] * PAGE + jnp.arange(PAGE)[None, :]
        valid = positions < length
        scores = jnp.einsum('thd,pkhd->pthk', request_query.astype(jnp.float32), page_keys, precision=highest) * scale
        same_page = variates[None, :, None] == cached_variates[:, None, :]
        scores = scores + jnp.where(same_page[:, :, None, :], same_bias[None, None, :, None], other_bias[None, None, :, None])
        keep = valid[:, None, None, :]
        page_max = lax.optimization_barrier(jnp.max(jnp.where(keep, scores, masked_score), axis=-1))
        weights = jnp.where(keep, jnp.exp(scores - page_max[..., None]), 0.0).astype(jnp.bfloat16)
        weights = lax.optimization_barrier(weights).astype(jnp.float32)
        page_total = lax.optimization_barrier(jnp.sum(weights, axis=-1))
        page_out = jnp.einsum('pthk,pkhd->pthd', weights, page_values, precision=highest)
        allowed = ancestry(parent_row)
        tree_scores = jnp.einsum('ihd,jhd->ihj', request_query.astype(jnp.float32), request_key.astype(jnp.float32), precision=highest) * scale
        same_tree = variates[:, None] == variates[None, :]
        tree_scores = tree_scores + jnp.where(same_tree[:, None, :], same_bias[None, :, None], other_bias[None, :, None])
        keep_tree = allowed[:, None, :]
        tree_max = lax.optimization_barrier(jnp.max(jnp.where(keep_tree, tree_scores, masked_score), axis=-1))
        tree_weights = jnp.where(keep_tree, jnp.exp(tree_scores - tree_max[..., None]), 0.0).astype(jnp.bfloat16)
        tree_weights = lax.optimization_barrier(tree_weights).astype(jnp.float32)
        tree_total = lax.optimization_barrier(jnp.sum(tree_weights, axis=-1))
        tree_out = jnp.einsum('ihj,jhd->ihd', tree_weights, request_value.astype(jnp.float32), precision=highest)
        overall = jnp.maximum(lax.optimization_barrier(jnp.max(page_max, axis=0)), tree_max)
        page_factor = jnp.exp(page_max - overall[None])
        tree_factor = jnp.exp(tree_max - overall)
        total = lax.optimization_barrier(jnp.sum(page_total * page_factor, axis=0)) + tree_total * tree_factor
        combined = lax.optimization_barrier(jnp.sum(page_out * page_factor[..., None], axis=0)) + tree_out * tree_factor[..., None]
        return (combined / total[..., None]).astype(jnp.bfloat16).reshape(TREE, QD)
    attended = lax.map(one_request, (query.reshape(REQUESTS, TREE, HEADS, HD), key_rows.reshape(REQUESTS, TREE, HEADS, HD), value_rows.reshape(REQUESTS, TREE, HEADS, HD), page_table, cache_len, parents, token_variates.reshape(REQUESTS, TREE)))
    attended = attended.reshape(TOKENS, QD)
    hidden_state = (tokens.astype(jnp.float32) + jnp.dot(attended, out_weight, preferred_element_type=jnp.float32)).astype(jnp.bfloat16)
    normed_two = rms_scaled(hidden_state, gains[1]).astype(jnp.bfloat16)
    gate = jnp.dot(normed_two, gate_up_weight[0], preferred_element_type=jnp.float32)
    upward = jnp.dot(normed_two, gate_up_weight[1], preferred_element_type=jnp.float32)
    activated = (jax.nn.silu(gate) * upward).astype(jnp.bfloat16)
    mixed = (hidden_state.astype(jnp.float32) + jnp.dot(activated, down_weight, preferred_element_type=jnp.float32)).astype(jnp.bfloat16)
    nodes = jnp.arange(TREE, dtype=jnp.int32)
    chosen = (accepted[:, :, None] == nodes[None, None, :]).astype(jnp.float32)
    new_keys = jnp.einsum('rat,rtq->raq', chosen, key_rows.reshape(REQUESTS, TREE, QD).astype(jnp.float32), precision=highest)
    new_values = jnp.einsum('rat,rtq->raq', chosen, value_rows.reshape(REQUESTS, TREE, QD).astype(jnp.float32), precision=highest)
    new_kv = jnp.stack([new_keys, new_values]).astype(jnp.bfloat16)
    return (mixed, attended, new_kv)
```

```python
import functools
import math

import jax
import jax.numpy as jnp
from jax import lax
from jax.experimental import pallas as pl
from jax.experimental.pallas import tpu as pltpu
from jax.sharding import PartitionSpec as P

HD = 64
NVAR = 4
TERMS = 3
BROWS = 16
epsilon = 1e-06
low = -1e30
f32 = jnp.float32
bf16 = jnp.bfloat16


def rms_scaled(values, gain):
    return values * lax.rsqrt(jnp.mean(values * values, axis=-1, keepdims=True) + epsilon) * gain


def iota(shape, dim):
    return lax.broadcasted_iota(jnp.int32, shape, dim)


def dot(a, b, ca=1, cb=0):
    return lax.dot_general(a, b, (((ca,), (cb,)), ((), ())), preferred_element_type=f32)


def kernel(
    R, H,
    tokens, gains, qkv_hbm, out_hbm, gu_hbm, down_hbm, vbias, cache_hbm, pvar, tvar, clen, ptab, parents, accepted,
    mixed, attended, new_kv,
    qkv, outw, gu, downw, pages, tbuf, qbuf, tvoh, bmat, oh, own_s, fill_s, own_rows, pm, plt, po,
    osend, ssend, obuf, sbuf, gbuf, act, hid, dsend, dbuf,
    lsem, ts, tr, qs, qr, os_, or_, ss, sr, gs, gr, ds_, dr,
):
    req = lax.axis_index("req")
    head = lax.axis_index("head")
    rows, D = tokens.shape
    QL = qkv.shape[2]
    HL = QL // HD
    pool, page = pvar.shape
    maxp = ptab.shape[1]
    tree = parents.shape[1]
    C = HL * tree
    FFL = gu.shape[2]

    def at_head(d):
        return {"req": req, "head": lax.rem(head + d, H)}

    def at_req(d):
        return {"req": lax.rem(req + d, R), "head": head}

    def remote(src, dst, s, r, device):
        return pltpu.make_async_remote_copy(
            src_ref=src, dst_ref=dst, send_sem=s, recv_sem=r, device_id=device, device_id_type=pl.DeviceIdType.MESH
        )

    barrier = pltpu.get_barrier_semaphore()
    for d in range(1, H):
        pl.semaphore_signal(barrier, inc=1, device_id=at_head(d), device_id_type=pl.DeviceIdType.MESH)

    @pl.loop(1, R)
    def _(d):
        pl.semaphore_signal(barrier, inc=1, device_id=at_req(d), device_id_type=pl.DeviceIdType.MESH)

    own_tokens = pltpu.make_async_copy(tokens, tbuf.at[head], lsem.at[0])
    own_tokens.start()
    get_qkv = pltpu.make_async_copy(qkv_hbm, qkv, lsem.at[1])
    get_qkv.start()
    get_pages = pltpu.make_async_copy(cache_hbm, pages, lsem.at[2])
    get_pages.start()
    get_out = pltpu.make_async_copy(out_hbm, outw, lsem.at[3])
    get_gu = pltpu.make_async_copy(gu_hbm, gu, lsem.at[4])
    get_down = pltpu.make_async_copy(down_hbm, downw, lsem.at[5])
    get_out.start()
    get_gu.start()
    get_down.start()
    pl.semaphore_wait(barrier, H - 1 + R - 1)

    token_copies = [
        remote(tokens, tbuf.at[head], ts.at[d - 1], tr.at[d - 1], at_head(d)) for d in range(1, H)
    ]
    for copy in token_copies:
        copy.start()

    table = ptab[...]
    place = iota(table.shape, 0) * maxp + iota(table.shape, 1) + 1
    row16 = iota((BROWS, page), 0)
    lane16 = iota((BROWS, page), 1)
    own_rows[...] = jnp.full(own_rows.shape, -1, jnp.int32)
    pm[...] = jnp.zeros(pm.shape, f32)
    plt[...] = jnp.zeros(plt.shape, f32)

    @pl.loop(0, pool)
    def _(p):
        code = jnp.max(jnp.where(table == req * pool + p, place, 0))
        used = code > 0
        slot = jnp.maximum(code - 1, 0)
        owner = slot // maxp
        filled = jnp.where(used, jnp.clip(clen[owner] - (slot - owner * maxp) * page, 0, page), 0)
        own_s[p] = owner
        fill_s[p] = filled
        own_rows[pl.ds(p, 1), :] = jnp.full((1, C), jnp.where(used, owner, -1), jnp.int32)
        line = pvar[pl.ds(p, 1), :]
        hot = jnp.where(row16 < TERMS * NVAR, (line == row16 % NVAR).astype(f32), 0.0)
        hot = jnp.where(row16 == TERMS * NVAR, (lane16 >= filled).astype(f32), hot)
        oh[p] = hot.astype(bf16)

    lane_head = iota((1, C), 1) // tree
    same_row = jnp.zeros((1, C), f32)
    other_row = jnp.zeros((1, C), f32)
    for h in range(HL):
        same_row = jnp.where(lane_head == h, vbias[0, head * HL + h], same_row)
        other_row = jnp.where(lane_head == h, vbias[1, head * HL + h], other_row)

    def split(row):
        one = row.astype(bf16).astype(f32)
        two = (row - one).astype(bf16).astype(f32)
        three = (row - one - two).astype(bf16).astype(f32)
        term = iota((BROWS, C), 0) // NVAR
        return jnp.where(term == 0, one, jnp.where(term == 1, two, jnp.where(term == 2, three, 0.0)))

    same_terms = split(same_row)
    other_terms = split(other_row)
    spread = (iota((tree, C), 0) == iota((tree, C), 1) % tree).astype(f32).astype(bf16)
    brow = iota((BROWS, C), 0)
    trow = iota((BROWS, tree), 0)
    for r in range(R):
        line = tvar[:, r * tree : (r + 1) * tree]
        hot = jnp.where(trow < TERMS * NVAR, (line == trow % NVAR).astype(f32), 0.0).astype(bf16)
        tvoh[r] = hot
        matched = dot(hot, spread) > 0.5
        terms = jnp.where(matched, same_terms, other_terms)
        bmat[r] = jnp.where(brow == TERMS * NVAR, low, terms).astype(bf16)

    up = parents[...]
    eye = (iota((tree, tree), 0) == iota((tree, tree), 1)).astype(f32)
    reach = ((iota((tree, tree), 0) == up).astype(f32) + eye).astype(bf16)
    clip = lambda v: jnp.minimum(v, 1.0).astype(bf16)
    reach2 = clip(dot(reach, reach))
    reach4 = clip(dot(reach2, reach2))
    reach8 = clip(dot(reach4, reach4))
    allowed = dot(reach8, spread) > 0.5

    block = (iota((C, QL), 0) // tree == iota((C, QL), 1) // HD).astype(f32).astype(bf16)

    own_tokens.wait()
    for copy in token_copies:
        copy.wait()
    get_qkv.wait()
    values = tbuf[...].astype(f32).reshape(H * rows, D)
    normed = rms_scaled(values, gains[0:1, :]).astype(bf16)
    scale = 1.0 / math.sqrt(HD)
    query = (dot(normed, qkv[0]).astype(bf16).astype(f32) * scale).astype(bf16)
    qbuf[req] = query

    def query_copy(d):
        return remote(qbuf.at[req], qbuf.at[req], qs.at[d], qr.at[d], at_req(d))

    @pl.loop(1, R)
    def _(d):
        query_copy(d).start()

    keys = dot(normed, qkv[1]).astype(bf16)
    vals = dot(normed, qkv[2]).astype(bf16)
    chosen = (iota((tree, accepted.shape[1]), 0) == accepted[...]).astype(f32).astype(bf16)
    new_kv[0, 0] = dot(chosen, keys, 0, 0).astype(bf16)
    new_kv[1, 0] = dot(chosen, vals, 0, 0).astype(bf16)

    def spread_query(q):
        return jnp.concatenate([q] * HL, axis=0) * block

    head_lanes = iota((HD, C), 1) // tree

    def pick(wide):
        out = wide[0:HD]
        for h in range(1, HL):
            out = jnp.where(head_lanes == h, wide[h * HD : (h + 1) * HD], out)
        return out

    tree_scores = dot(keys, spread_query(query), 1, 1) + dot(tvoh[req], bmat[req], 0, 0)
    tree_max = jnp.max(jnp.where(allowed, tree_scores, low), axis=0, keepdims=True)
    tree_w = jnp.where(allowed, jnp.exp(tree_scores - tree_max), 0.0).astype(bf16)
    tree_total = jnp.sum(tree_w.astype(f32), axis=0, keepdims=True)
    tree_out = pick(dot(vals, tree_w, 0, 0))

    get_pages.wait()

    @pl.loop(1, R)
    def _(d):
        query_copy(d).wait()

    group = 4 if pool % 4 == 0 else 1

    @pl.loop(0, pool // group)
    def _(g):
        for k in range(group):
            p = g * group + k
            owner = own_s[p]
            scores = dot(pages[0, p], spread_query(qbuf[owner]), 1, 1) + dot(oh[p], bmat[owner], 0, 0)
            top = jnp.max(scores, axis=0, keepdims=True)
            w = jnp.exp(scores - top).astype(bf16)
            pm[pl.ds(p, 1), :] = top
            plt[pl.ds(p, 1), :] = jnp.sum(w.astype(f32), axis=0, keepdims=True)
            po[p] = pick(dot(pages[1, p], w, 0, 0))

    def out_copy(d):
        return remote(osend.at[d], obuf.at[d], os_.at[d], or_.at[d], at_req(d))

    def stat_copy(d):
        return remote(ssend.at[d], sbuf.at[d], ss.at[d], sr.at[d], at_req(d))

    def merged(r):
        mask = own_rows[...] == r
        maxes = pm[...]
        top = jnp.max(jnp.where(mask, maxes, low), axis=0, keepdims=True)
        factor = jnp.where(mask, jnp.exp(maxes - top), 0.0)
        total = jnp.sum(factor * plt[...], axis=0, keepdims=True)
        out = factor[0:1] * po[0]
        for p in range(1, pool):
            out = out + factor[p : p + 1] * po[p]
        return top, total, out

    srow = iota((8, C), 0)

    @pl.loop(1, R)
    def _(d):
        top, total, out = merged(lax.rem(req + d, R))
        osend[d] = out.astype(bf16)
        ssend[d] = jnp.where(srow == 0, top, total)
        out_copy(d).start()
        stat_copy(d).start()

    top, total, out = merged(req)
    new_top = jnp.maximum(top, tree_max)
    fa = jnp.exp(top - new_top)
    fb = jnp.exp(tree_max - new_top)
    osend[0] = jnp.zeros((HD, C), bf16)
    total = total * fa + tree_total * fb
    out = out * fa + tree_out * fb
    top = new_top

    @pl.loop(1, R)
    def _(d):
        out_copy(d).wait()
        stat_copy(d).wait()

    final_top = top
    for d in range(1, R):
        final_top = jnp.maximum(final_top, sbuf[d][0:1])
    fa = jnp.exp(top - final_top)
    total = total * fa
    out = out * fa
    for d in range(1, R):
        stats = sbuf[d]
        fd = jnp.exp(stats[0:1] - final_top)
        total = total + stats[1:2] * fd
        out = out + obuf[d].astype(f32) * fd
    att_t = (out / total).astype(bf16)
    diag = jnp.concatenate([att_t] * HL, axis=0) * (
        iota((HL * HD, C), 0) // HD == iota((HL * HD, C), 1) // tree
    ).astype(f32).astype(bf16)
    att = dot(spread, diag, 1, 1).astype(bf16)
    gbuf[head] = att
    att_copies = [remote(gbuf.at[head], gbuf.at[head], gs.at[d - 1], gr.at[d - 1], at_head(d)) for d in range(1, H)]
    for copy in att_copies:
        copy.start()
    attended[...] = att
    get_out.wait()
    state = values + dot(att, outw[pl.ds(pl.multiple_of(head * QL, QL), QL), :])
    for d in range(1, H):
        att_copies[d - 1].wait()
        source = lax.rem(head + H - d, H)
        state = state + dot(gbuf[source], outw[pl.ds(pl.multiple_of(source * QL, QL), QL), :])
    state = state.astype(bf16).astype(f32)
    hid[...] = state.reshape(H, rows, D)
    normed_two = rms_scaled(state, gains[1:2, :]).astype(bf16)
    get_gu.wait()
    step = 256
    for c in range(0, FFL, step):
        gate = dot(normed_two, gu[0, :, c : c + step])
        upward = dot(normed_two, gu[1, :, c : c + step])
        act[:, c : c + step] = (gate / (1.0 + jnp.exp(-gate)) * upward).astype(bf16)
    get_down.wait()
    activated = act[...]
    for c in range(0, D, step):
        part = dot(activated, downw[:, c : c + step])
        dsend[:, :, c : c + step] = part.reshape(H, rows, step).astype(bf16)
    down_copies = [
        remote(dsend.at[lax.rem(head + d, H)], dbuf.at[d - 1], ds_.at[d - 1], dr.at[d - 1], at_head(d))
        for d in range(1, H)
    ]
    for copy in down_copies:
        copy.start()
    result = dsend[head].astype(f32)
    for d in range(1, H):
        down_copies[d - 1].wait()
        result = result + dbuf[d - 1].astype(f32)
    mixed[...] = (hid[head] + result).astype(bf16)


def shards(
    tokens, gains, qkv_weight, out_weight, gate_up_weight, down_weight, variate_bias, page_cache, page_variates,
    token_variates, cache_len, page_table, parents, accepted,
):
    R = lax.axis_size("req")
    H = lax.axis_size("head")
    rows, D = tokens.shape
    QL = qkv_weight.shape[2]
    HL = QL // HD
    pool, page = page_variates.shape
    tree = parents.shape[1]
    C = HL * tree
    padded = (pool + 7) // 8 * 8
    hbm = pl.BlockSpec(memory_space=pl.ANY)
    vmem = pl.BlockSpec(memory_space=pltpu.VMEM)
    smem = pl.BlockSpec(memory_space=pltpu.SMEM)
    dma = pltpu.SemaphoreType.DMA
    return tuple(pl.pallas_call(
        functools.partial(kernel, R, H),
        out_shape=(
            jax.ShapeDtypeStruct((rows, D), bf16),
            jax.ShapeDtypeStruct((tree, QL), bf16),
            jax.ShapeDtypeStruct((2, 1, accepted.shape[1], QL), bf16),
        ),
        in_specs=[hbm, vmem, hbm, hbm, hbm, hbm, smem, hbm, vmem, vmem, smem, vmem, vmem, vmem],
        out_specs=(vmem, vmem, vmem),
        scratch_shapes=[
            pltpu.VMEM(qkv_weight.shape, bf16),
            pltpu.VMEM(out_weight.shape, bf16),
            pltpu.VMEM(gate_up_weight.shape, bf16),
            pltpu.VMEM(down_weight.shape, bf16),
            pltpu.VMEM(page_cache.shape, bf16),
            pltpu.VMEM((H, rows, D), bf16),
            pltpu.VMEM((R, tree, QL), bf16),
            pltpu.VMEM((R, BROWS, tree), bf16),
            pltpu.VMEM((R, BROWS, C), bf16),
            pltpu.VMEM((pool, BROWS, page), bf16),
            pltpu.SMEM((pool,), jnp.int32),
            pltpu.SMEM((pool,), jnp.int32),
            pltpu.VMEM((padded, C), jnp.int32),
            pltpu.VMEM((padded, C), f32),
            pltpu.VMEM((padded, C), f32),
            pltpu.VMEM((pool, HD, C), f32),
            pltpu.VMEM((R, HD, C), bf16),
            pltpu.VMEM((R, 8, C), f32),
            pltpu.VMEM((R, HD, C), bf16),
            pltpu.VMEM((R, 8, C), f32),
            pltpu.VMEM((H, tree, QL), bf16),
            pltpu.VMEM((tree, gate_up_weight.shape[2]), bf16),
            pltpu.VMEM((H, rows, D), f32),
            pltpu.VMEM((H, rows, D), bf16),
            pltpu.VMEM((H, rows, D), bf16),
            dma((6,)),
            dma((H,)), dma((H,)),
            dma((R,)), dma((R,)),
            dma((R,)), dma((R,)),
            dma((R,)), dma((R,)),
            dma((H,)), dma((H,)),
            dma((H,)), dma((H,)),
        ],
        compiler_params=pltpu.CompilerParams(
            collective_id=0, has_side_effects=True, vmem_limit_bytes=52 * 1024 * 1024
        ),
        cost_estimate=pl.CostEstimate(flops=10**9, bytes_accessed=12 * 10**6, transcendentals=10**6),
    )(
        tokens, gains, qkv_weight, out_weight, gate_up_weight, down_weight, variate_bias, page_cache, page_variates,
        token_variates.reshape(1, -1), cache_len, page_table, parents, accepted,
    ))


def solution(mesh):
    return jax.shard_map(
        shards,
        mesh=mesh,
        in_specs=(
            P(("req", "head"), None),
            P(),
            P(None, None, "head"),
            P(),
            P(None, None, "head"),
            P("head", None),
            P(),
            P(None, "req", None, "head"),
            P("req", None),
            P(),
            P(),
            P(),
            P("req", None),
            P("req", None),
        ),
        out_specs=(P(("req", "head"), None), P("req", "head"), P(None, "req", None, "head")),
        check_vma=False,
    )
```

```python
import functools
import math

import jax
import jax.numpy as jnp
from jax import lax
from jax.experimental import pallas as pl
from jax.experimental.pallas import tpu as pltpu
from jax.sharding import PartitionSpec as P

HD = 64
NVAR = 4
TERMS = 3
BROWS = 16
epsilon = 1e-06
low = -1e30
f32 = jnp.float32
bf16 = jnp.bfloat16


def rms_scaled(values, gain):
    return values * lax.rsqrt(jnp.mean(values * values, axis=-1, keepdims=True) + epsilon) * gain


def iota(shape, dim):
    return lax.broadcasted_iota(jnp.int32, shape, dim)


def dot(a, b, ca=1, cb=0):
    return lax.dot_general(a, b, (((ca,), (cb,)), ((), ())), preferred_element_type=f32)


def kernel(
    R, H,
    tokens, gains_hbm, qkv_hbm, out_hbm, gu_hbm, down_hbm, vbias_hbm, cache_hbm, pvar_hbm, tvar_hbm, clen_hbm,
    ptab_hbm, parents_hbm, accepted_hbm,
    mixed, attended, new_kv,
    gains, vbias, pvar, tvar, clen, ptab, parents, accepted, vt,
    qkv, outw, gu, downw, pages, tbuf, qbuf, tvoh, bmat, oh, own_s, own_rows, pm, plt, po,
    osend, ssend, obuf, sbuf, gbuf, act, hid, dsend, dbuf,
    lsem, ksem, ts, tr, qs, qr, fs, fr, os_, or_, ss, sr, gs, gr, ds_, dr,
):
    req = lax.axis_index("req")
    head = lax.axis_index("head")
    rows, D = tokens.shape
    QL = qkv.shape[2]
    HL = QL // HD
    pool, page = pvar.shape
    maxp = ptab.shape[1]
    tree = parents.shape[1]
    C = HL * tree
    FFL = gu.shape[2]

    def at_head(d):
        return {"req": req, "head": lax.rem(head + d, H)}

    def at_req(d):
        return {"req": lax.rem(req + d, R), "head": head}

    def remote(src, dst, s, r, device):
        return pltpu.make_async_remote_copy(
            src_ref=src, dst_ref=dst, send_sem=s, recv_sem=r, device_id=device, device_id_type=pl.DeviceIdType.MESH
        )

    barrier = pltpu.get_barrier_semaphore()
    for d in range(1, H):
        pl.semaphore_signal(barrier, inc=1, device_id=at_head(d), device_id_type=pl.DeviceIdType.MESH)

    @pl.loop(1, R)
    def _(d):
        pl.semaphore_signal(barrier, inc=1, device_id=at_req(d), device_id_type=pl.DeviceIdType.MESH)

    small = [
        pltpu.make_async_copy(src, dst, ksem.at[k])
        for k, (src, dst) in enumerate((
            (ptab_hbm, ptab), (pvar_hbm, pvar), (clen_hbm, clen), (tvar_hbm, tvar), (vbias_hbm, vbias),
            (parents_hbm, parents), (accepted_hbm, accepted), (gains_hbm, gains),
        ))
    ]
    for copy in small:
        copy.start()
    own_tokens = pltpu.make_async_copy(tokens, tbuf.at[head], lsem.at[0])
    own_tokens.start()
    get_qkv = pltpu.make_async_copy(qkv_hbm, qkv, lsem.at[1])
    get_qkv.start()
    get_pages = pltpu.make_async_copy(cache_hbm, pages, lsem.at[2])
    get_pages.start()
    get_out = pltpu.make_async_copy(out_hbm, outw, lsem.at[3])
    get_gu = pltpu.make_async_copy(gu_hbm, gu, lsem.at[4])
    get_down = pltpu.make_async_copy(down_hbm, downw, lsem.at[5])
    get_out.start()
    get_gu.start()
    get_down.start()
    pl.semaphore_wait(barrier, H - 1 + R - 1)

    token_copies = [
        remote(tokens, tbuf.at[head], ts.at[d - 1], tr.at[d - 1], at_head(d)) for d in range(1, H)
    ]
    for copy in token_copies:
        copy.start()

    for copy in small:
        copy.wait()
    table = ptab[...]
    place = iota(table.shape, 0) * maxp + iota(table.shape, 1) + 1
    row16 = iota((BROWS, page), 0)
    lane16 = iota((BROWS, page), 1)
    own_rows[...] = jnp.full(own_rows.shape, -1, jnp.int32)
    pm[...] = jnp.zeros(pm.shape, f32)
    plt[...] = jnp.zeros(plt.shape, f32)

    group = 4 if pool % 4 == 0 else 1

    @pl.loop(0, pool // group)
    def _(g):
        for k in range(group):
            p = g * group + k
            code = jnp.max(jnp.where(table == req * pool + p, place, 0))
            used = code > 0
            slot = jnp.maximum(code - 1, 0)
            owner = slot // maxp
            filled = jnp.where(used, jnp.clip(clen[owner] - (slot - owner * maxp) * page, 0, page), 0)
            own_s[p] = owner
            own_rows[pl.ds(p, 1), :] = jnp.full((1, C), jnp.where(used, owner, -1), jnp.int32)
            line = pvar[pl.ds(p, 1), :]
            hot = jnp.where(row16 < TERMS * NVAR, (line == row16 % NVAR).astype(f32), 0.0)
            hot = jnp.where(row16 == TERMS * NVAR, (lane16 >= filled).astype(f32), hot)
            oh[p] = hot.astype(bf16)

    own_tokens.wait()
    for copy in token_copies:
        copy.wait()
    get_qkv.wait()
    values = tbuf[...].astype(f32).reshape(H * rows, D)
    normed = rms_scaled(values, gains[0:1, :]).astype(bf16)
    scale = 1.0 / math.sqrt(HD)
    query = (dot(normed, qkv[0]).astype(bf16).astype(f32) * scale).astype(bf16)
    qbuf[req] = query

    half = R // 2
    partner = req + 1 - 2 * lax.rem(req, 2)
    beside = {"req": partner, "head": head}

    def query_copy(k):
        return remote(qbuf.at[req], qbuf.at[req], qs.at[k], qr.at[k], at_req(2 * k))

    def forward_copy(k):
        source = lax.rem(req + R - 2 * k, R)
        return remote(qbuf.at[source], qbuf.at[source], fs.at[k], fr.at[k], beside)

    @pl.loop(1, half)
    def _(k):
        query_copy(k).start()

    forward_copy(0).start()

    keys = dot(normed, qkv[1]).astype(bf16)
    vals = dot(normed, qkv[2]).astype(bf16)
    chosen = (iota((tree, accepted.shape[1]), 0) == accepted[...]).astype(f32).astype(bf16)
    new_kv[0, 0] = dot(chosen, keys, 0, 0).astype(bf16)
    new_kv[1, 0] = dot(chosen, vals, 0, 0).astype(bf16)

    lane_head = iota((1, C), 1) // tree
    same_row = jnp.zeros((1, C), f32)
    other_row = jnp.zeros((1, C), f32)
    for h in range(HL):
        same_row = jnp.where(lane_head == h, vbias[0, head * HL + h], same_row)
        other_row = jnp.where(lane_head == h, vbias[1, head * HL + h], other_row)

    def split(row):
        one = row.astype(bf16).astype(f32)
        two = (row - one).astype(bf16).astype(f32)
        three = (row - one - two).astype(bf16).astype(f32)
        term = iota((BROWS, C), 0) // NVAR
        return jnp.where(term == 0, one, jnp.where(term == 1, two, jnp.where(term == 2, three, 0.0)))

    same_terms = split(same_row)
    other_terms = split(other_row)
    spread = (iota((tree, C), 0) == iota((tree, C), 1) % tree).astype(f32).astype(bf16)
    brow = iota((BROWS, C), 0)
    trow = iota((BROWS, tree), 0)
    for r in range(R):
        line = tvar[:, r * tree : (r + 1) * tree]
        hot = jnp.where(trow < TERMS * NVAR, (line == trow % NVAR).astype(f32), 0.0).astype(bf16)
        tvoh[r] = hot
        matched = dot(hot, spread) > 0.5
        terms = jnp.where(matched, same_terms, other_terms)
        bmat[r] = jnp.where(brow == TERMS * NVAR, low, terms).astype(bf16)

    up = parents[...]
    eye = (iota((tree, tree), 0) == iota((tree, tree), 1)).astype(f32)
    reach = ((iota((tree, tree), 0) == up).astype(f32) + eye).astype(bf16)
    clip = lambda v: jnp.minimum(v, 1.0).astype(bf16)
    reach2 = clip(dot(reach, reach))
    reach4 = clip(dot(reach2, reach2))
    reach8 = clip(dot(reach4, reach4))
    allowed = dot(reach8, spread) > 0.5

    block = (iota((C, QL), 0) // tree == iota((C, QL), 1) // HD).astype(f32).astype(bf16)

    @pl.loop(1, half)
    def _(k):
        query_copy(k).wait()
        forward_copy(k).start()

    def spread_query(q):
        return jnp.concatenate([q] * HL, axis=0) * block

    head_lanes = iota((HD, C), 1) // tree

    def pick(wide):
        out = wide[0:HD]
        for h in range(1, HL):
            out = jnp.where(head_lanes == h, wide[h * HD : (h + 1) * HD], out)
        return out

    tree_scores = dot(keys, spread_query(query), 1, 1) + dot(tvoh[req], bmat[req], 0, 0)
    tree_max = jnp.max(jnp.where(allowed, tree_scores, low), axis=0, keepdims=True)
    tree_w = jnp.where(allowed, jnp.exp(tree_scores - tree_max), 0.0).astype(bf16)
    tree_total = jnp.sum(tree_w.astype(f32), axis=0, keepdims=True)
    tree_out = pick(dot(vals, tree_w, 0, 0))

    get_pages.wait()

    @pl.loop(0, pool // group)
    def _(g):
        for k in range(group):
            vt[g * group + k] = pages[1, g * group + k].T

    @pl.loop(0, half)
    def _(k):
        forward_copy(k).wait()

    @pl.loop(0, pool // group)
    def _(g):
        for k in range(group):
            p = g * group + k
            owner = own_s[p]
            scores = dot(pages[0, p], spread_query(qbuf[owner]), 1, 1) + dot(oh[p], bmat[owner], 0, 0)
            top = jnp.max(scores, axis=0, keepdims=True)
            w = jnp.exp(scores - top).astype(bf16)
            pm[pl.ds(p, 1), :] = top
            plt[pl.ds(p, 1), :] = jnp.sum(w.astype(f32), axis=0, keepdims=True)
            po[p] = pick(dot(vt[p], w))

    def out_copy(d):
        return remote(osend.at[d], obuf.at[d], os_.at[d], or_.at[d], at_req(d))

    def stat_copy(d):
        return remote(ssend.at[d], sbuf.at[d], ss.at[d], sr.at[d], at_req(d))

    def merged(r):
        mask = own_rows[...] == r
        maxes = pm[...]
        top = jnp.max(jnp.where(mask, maxes, low), axis=0, keepdims=True)
        factor = jnp.where(mask, jnp.exp(maxes - top), 0.0)
        total = jnp.sum(factor * plt[...], axis=0, keepdims=True)
        out = factor[0:1] * po[0]
        for p in range(1, pool):
            out = out + factor[p : p + 1] * po[p]
        return top, total, out

    srow = iota((8, C), 0)

    @pl.loop(1, R)
    def _(d):
        top, total, out = merged(lax.rem(req + d, R))
        osend[d] = out.astype(bf16)
        ssend[d] = jnp.where(srow == 0, top, total)
        out_copy(d).start()
        stat_copy(d).start()

    top, total, out = merged(req)
    new_top = jnp.maximum(top, tree_max)
    fa = jnp.exp(top - new_top)
    fb = jnp.exp(tree_max - new_top)
    osend[0] = jnp.zeros((HD, C), bf16)
    total = total * fa + tree_total * fb
    out = out * fa + tree_out * fb
    top = new_top

    @pl.loop(1, R)
    def _(d):
        out_copy(d).wait()
        stat_copy(d).wait()

    final_top = top
    for d in range(1, R):
        final_top = jnp.maximum(final_top, sbuf[d][0:1])
    fa = jnp.exp(top - final_top)
    total = total * fa
    out = out * fa
    for d in range(1, R):
        stats = sbuf[d]
        fd = jnp.exp(stats[0:1] - final_top)
        total = total + stats[1:2] * fd
        out = out + obuf[d].astype(f32) * fd
    att_t = (out / total).astype(bf16)
    diag = jnp.concatenate([att_t] * HL, axis=0) * (
        iota((HL * HD, C), 0) // HD == iota((HL * HD, C), 1) // tree
    ).astype(f32).astype(bf16)
    att = dot(spread, diag, 1, 1).astype(bf16)
    gbuf[head] = att
    att_copies = [remote(gbuf.at[head], gbuf.at[head], gs.at[d - 1], gr.at[d - 1], at_head(d)) for d in range(1, H)]
    for copy in att_copies:
        copy.start()
    attended[...] = att
    get_out.wait()
    state = values + dot(att, outw[pl.ds(pl.multiple_of(head * QL, QL), QL), :])
    for d in range(1, H):
        att_copies[d - 1].wait()
        source = lax.rem(head + H - d, H)
        state = state + dot(gbuf[source], outw[pl.ds(pl.multiple_of(source * QL, QL), QL), :])
    state = state.astype(bf16).astype(f32)
    hid[...] = state.reshape(H, rows, D)
    normed_two = rms_scaled(state, gains[1:2, :]).astype(bf16)
    get_gu.wait()
    step = 256
    for c in range(0, FFL, step):
        gate = dot(normed_two, gu[0, :, c : c + step])
        upward = dot(normed_two, gu[1, :, c : c + step])
        act[:, c : c + step] = (gate / (1.0 + jnp.exp(-gate)) * upward).astype(bf16)
    get_down.wait()
    activated = act[...]
    for c in range(0, D, step):
        part = dot(activated, downw[:, c : c + step])
        dsend[:, :, c : c + step] = part.reshape(H, rows, step).astype(bf16)
    down_copies = [
        remote(dsend.at[lax.rem(head + d, H)], dbuf.at[d - 1], ds_.at[d - 1], dr.at[d - 1], at_head(d))
        for d in range(1, H)
    ]
    for copy in down_copies:
        copy.start()
    result = dsend[head].astype(f32)
    for d in range(1, H):
        down_copies[d - 1].wait()
        result = result + dbuf[d - 1].astype(f32)
    mixed[...] = (hid[head] + result).astype(bf16)


def hand_over(mixed, attended, new_kv, mixed_out, attended_out, new_kv_out, sem):
    copies = [
        pltpu.make_async_copy(src, dst, sem.at[k])
        for k, (src, dst) in enumerate(((mixed, mixed_out), (attended, attended_out), (new_kv, new_kv_out)))
    ]
    for copy in copies:
        copy.start()
    for copy in copies:
        copy.wait()


def shards(
    tokens, gains, qkv_weight, out_weight, gate_up_weight, down_weight, variate_bias, page_cache, page_variates,
    token_variates, cache_len, page_table, parents, accepted,
):
    R = lax.axis_size("req")
    H = lax.axis_size("head")
    rows, D = tokens.shape
    QL = qkv_weight.shape[2]
    HL = QL // HD
    pool, page = page_variates.shape
    tree = parents.shape[1]
    C = HL * tree
    padded = (pool + 7) // 8 * 8
    hbm = pl.BlockSpec(memory_space=pl.ANY)
    vmem = pl.BlockSpec(memory_space=pltpu.VMEM)
    dma = pltpu.SemaphoreType.DMA
    results = pl.pallas_call(
        functools.partial(kernel, R, H),
        out_shape=(
            jax.ShapeDtypeStruct((rows, D), bf16),
            jax.ShapeDtypeStruct((tree, QL), bf16),
            jax.ShapeDtypeStruct((2, 1, accepted.shape[1], QL), bf16),
        ),
        in_specs=[hbm] * 14,
        out_specs=(vmem, vmem, vmem),
        scratch_shapes=[
            pltpu.VMEM(gains.shape, f32),
            pltpu.SMEM(variate_bias.shape, f32),
            pltpu.VMEM(page_variates.shape, jnp.int32),
            pltpu.VMEM((1, token_variates.shape[0]), jnp.int32),
            pltpu.SMEM(cache_len.shape, jnp.int32),
            pltpu.VMEM(page_table.shape, jnp.int32),
            pltpu.VMEM(parents.shape, jnp.int32),
            pltpu.VMEM(accepted.shape, jnp.int32),
            pltpu.VMEM((pool, QL, page), bf16),
            pltpu.VMEM(qkv_weight.shape, bf16),
            pltpu.VMEM(out_weight.shape, bf16),
            pltpu.VMEM(gate_up_weight.shape, bf16),
            pltpu.VMEM(down_weight.shape, bf16),
            pltpu.VMEM(page_cache.shape, bf16),
            pltpu.VMEM((H, rows, D), bf16),
            pltpu.VMEM((R, tree, QL), bf16),
            pltpu.VMEM((R, BROWS, tree), bf16),
            pltpu.VMEM((R, BROWS, C), bf16),
            pltpu.VMEM((pool, BROWS, page), bf16),
            pltpu.SMEM((pool,), jnp.int32),
            pltpu.VMEM((padded, C), jnp.int32),
            pltpu.VMEM((padded, C), f32),
            pltpu.VMEM((padded, C), f32),
            pltpu.VMEM((pool, HD, C), f32),
            pltpu.VMEM((R, HD, C), bf16),
            pltpu.VMEM((R, 8, C), f32),
            pltpu.VMEM((R, HD, C), bf16),
            pltpu.VMEM((R, 8, C), f32),
            pltpu.VMEM((H, tree, QL), bf16),
            pltpu.VMEM((tree, gate_up_weight.shape[2]), bf16),
            pltpu.VMEM((H, rows, D), f32),
            pltpu.VMEM((H, rows, D), bf16),
            pltpu.VMEM((H, rows, D), bf16),
            dma((6,)),
            dma((8,)),
            dma((H,)), dma((H,)),
            dma((R,)), dma((R,)),
            dma((R,)), dma((R,)),
            dma((R,)), dma((R,)),
            dma((R,)), dma((R,)),
            dma((H,)), dma((H,)),
            dma((H,)), dma((H,)),
        ],
        compiler_params=pltpu.CompilerParams(
            collective_id=0, has_side_effects=True, vmem_limit_bytes=60 * 1024 * 1024
        ),
        cost_estimate=pl.CostEstimate(flops=10**9, bytes_accessed=12 * 10**6, transcendentals=10**6),
    )(
        tokens, gains, qkv_weight, out_weight, gate_up_weight, down_weight, variate_bias, page_cache, page_variates,
        token_variates.reshape(1, -1), cache_len, page_table, parents, accepted,
    )
    return tuple(pl.pallas_call(
        hand_over,
        out_shape=tuple(jax.ShapeDtypeStruct(a.shape, a.dtype) for a in results),
        in_specs=[hbm] * 3,
        out_specs=(hbm,) * 3,
        scratch_shapes=[dma((3,))],
        compiler_params=pltpu.CompilerParams(vmem_limit_bytes=60 * 1024 * 1024),
    )(*results))


def solution(mesh):
    return jax.shard_map(
        shards,
        mesh=mesh,
        in_specs=(
            P(("req", "head"), None),
            P(),
            P(None, None, "head"),
            P(),
            P(None, None, "head"),
            P("head", None),
            P(),
            P(None, "req", None, "head"),
            P("req", None),
            P(),
            P(),
            P(),
            P("req", None),
            P("req", None),
        ),
        out_specs=(P(("req", "head"), None), P("req", "head"), P(None, "req", None, "head")),
        check_vma=False,
    )
```

```python
import functools
import math

import jax
import jax.numpy as jnp
from jax import lax
from jax.experimental import pallas as pl
from jax.experimental.pallas import tpu as pltpu
from jax.sharding import PartitionSpec as P

HD = 64
NVAR = 4
TERMS = 3
BROWS = 16
STEP = 256
epsilon = 1e-06
low = -1e30
f32 = jnp.float32
bf16 = jnp.bfloat16


def rms_scaled(values, gain):
    return values * lax.rsqrt(jnp.mean(values * values, axis=-1, keepdims=True) + epsilon) * gain


def iota(shape, dim):
    return lax.broadcasted_iota(jnp.int32, shape, dim)


def dot(a, b, ca=1, cb=0):
    return lax.dot_general(a, b, (((ca,), (cb,)), ((), ())), preferred_element_type=f32)


def kernel(
    R, H,
    tokens, gains_hbm, qkv_hbm, out_hbm, gu_hbm, down_hbm, vbias_hbm, cache_hbm, pvar_hbm, tvar_hbm, clen_hbm,
    ptab_hbm, parents_hbm, accepted_hbm,
    mixed, attended, new_kv,
    gains, vbias, pvar, tvar, clen, ptab, parents, accepted, vt,
    qkv, outw, gu, downw, pages, tbuf, qbuf, tvoh, bmat, oh, own_s, own_rows, pm, plt, po,
    osend, ssend, obuf, sbuf, gbuf, act, hid, dsend, dbuf,
    lsem, ksem, ts, tr, qs, qr, fs, fr, os_, or_, ss, sr, gs, gr, ds_, dr,
):
    req = lax.axis_index("req")
    head = lax.axis_index("head")
    rows, D = tokens.shape
    QL = qkv.shape[2]
    HL = QL // HD
    pool, page = pvar.shape
    maxp = ptab.shape[1]
    tree = parents.shape[1]
    C = HL * tree
    FFL = gu.shape[2]

    def at_head(d):
        return {"req": req, "head": lax.rem(head + d, H)}

    def at_req(d):
        return {"req": lax.rem(req + d, R), "head": head}

    def remote(src, dst, s, r, device):
        return pltpu.make_async_remote_copy(
            src_ref=src, dst_ref=dst, send_sem=s, recv_sem=r, device_id=device, device_id_type=pl.DeviceIdType.MESH
        )

    barrier = pltpu.get_barrier_semaphore()
    for d in range(1, H):
        pl.semaphore_signal(barrier, inc=1, device_id=at_head(d), device_id_type=pl.DeviceIdType.MESH)

    @pl.loop(1, R)
    def _(d):
        pl.semaphore_signal(barrier, inc=1, device_id=at_req(d), device_id_type=pl.DeviceIdType.MESH)

    small = [
        pltpu.make_async_copy(src, dst, ksem.at[k])
        for k, (src, dst) in enumerate((
            (ptab_hbm, ptab), (pvar_hbm, pvar), (clen_hbm, clen), (tvar_hbm, tvar), (vbias_hbm, vbias),
            (parents_hbm, parents), (accepted_hbm, accepted), (gains_hbm, gains),
        ))
    ]
    for copy in small:
        copy.start()
    own_tokens = pltpu.make_async_copy(tokens, tbuf.at[head], lsem.at[0])
    own_tokens.start()
    get_qkv = pltpu.make_async_copy(qkv_hbm, qkv, lsem.at[1])
    get_qkv.start()
    get_pages = pltpu.make_async_copy(cache_hbm, pages, lsem.at[2])
    get_pages.start()
    get_out = pltpu.make_async_copy(out_hbm, outw, lsem.at[3])
    get_gu = pltpu.make_async_copy(gu_hbm, gu, lsem.at[4])
    get_down = pltpu.make_async_copy(down_hbm, downw, lsem.at[5])
    get_out.start()
    get_gu.start()
    get_down.start()
    pl.semaphore_wait(barrier, H - 1 + R - 1)

    token_copies = [
        remote(tokens, tbuf.at[head], ts.at[d - 1], tr.at[d - 1], at_head(d)) for d in range(1, H)
    ]
    for copy in token_copies:
        copy.start()

    for copy in small:
        copy.wait()
    table = ptab[...]
    place = iota(table.shape, 0) * maxp + iota(table.shape, 1) + 1
    row16 = iota((BROWS, page), 0)
    lane16 = iota((BROWS, page), 1)
    own_rows[...] = jnp.full(own_rows.shape, -1, jnp.int32)
    pm[...] = jnp.zeros(pm.shape, f32)
    plt[...] = jnp.zeros(plt.shape, f32)

    group = 4 if pool % 4 == 0 else 1

    @pl.loop(0, pool // group)
    def _(g):
        for k in range(group):
            p = g * group + k
            code = jnp.max(jnp.where(table == req * pool + p, place, 0))
            used = code > 0
            slot = jnp.maximum(code - 1, 0)
            owner = slot // maxp
            filled = jnp.where(used, jnp.clip(clen[owner] - (slot - owner * maxp) * page, 0, page), 0)
            own_s[p] = owner
            own_rows[pl.ds(p, 1), :] = jnp.full((1, C), jnp.where(used, owner, -1), jnp.int32)
            line = pvar[pl.ds(p, 1), :]
            hot = jnp.where(row16 < TERMS * NVAR, (line == row16 % NVAR).astype(f32), 0.0)
            hot = jnp.where(row16 == TERMS * NVAR, (lane16 >= filled).astype(f32), hot)
            oh[p] = hot.astype(bf16)

    own_tokens.wait()
    for copy in token_copies:
        copy.wait()
    get_qkv.wait()
    values = tbuf[...].astype(f32).reshape(H * rows, D)
    normed = rms_scaled(values, gains[0:1, :]).astype(bf16)
    scale = 1.0 / math.sqrt(HD)
    query = (dot(normed, qkv[0]).astype(bf16).astype(f32) * scale).astype(bf16)
    qbuf[req] = query

    half = R // 2
    partner = req + 1 - 2 * lax.rem(req, 2)
    beside = {"req": partner, "head": head}

    def query_copy(k):
        return remote(qbuf.at[req], qbuf.at[req], qs.at[k], qr.at[k], at_req(2 * k))

    def forward_copy(k):
        source = lax.rem(req + R - 2 * k, R)
        return remote(qbuf.at[source], qbuf.at[source], fs.at[k], fr.at[k], beside)

    @pl.loop(1, half)
    def _(k):
        query_copy(k).start()

    forward_copy(0).start()

    keys = dot(normed, qkv[1]).astype(bf16)
    vals = dot(normed, qkv[2]).astype(bf16)
    chosen = (iota((tree, accepted.shape[1]), 0) == accepted[...]).astype(f32).astype(bf16)
    new_kv[0, 0] = dot(chosen, keys, 0, 0).astype(bf16)
    new_kv[1, 0] = dot(chosen, vals, 0, 0).astype(bf16)

    @pl.loop(1, half)
    def _(k):
        query_copy(k).wait()
        forward_copy(k).start()

    lane_head = iota((1, C), 1) // tree
    same_row = jnp.zeros((1, C), f32)
    other_row = jnp.zeros((1, C), f32)
    for h in range(HL):
        same_row = jnp.where(lane_head == h, vbias[0, head * HL + h], same_row)
        other_row = jnp.where(lane_head == h, vbias[1, head * HL + h], other_row)

    def split(row):
        one = row.astype(bf16).astype(f32)
        two = (row - one).astype(bf16).astype(f32)
        three = (row - one - two).astype(bf16).astype(f32)
        term = iota((BROWS, C), 0) // NVAR
        return jnp.where(term == 0, one, jnp.where(term == 1, two, jnp.where(term == 2, three, 0.0)))

    same_terms = split(same_row)
    other_terms = split(other_row)
    spread = (iota((tree, C), 0) == iota((tree, C), 1) % tree).astype(f32).astype(bf16)
    brow = iota((BROWS, C), 0)
    trow = iota((BROWS, tree), 0)
    for r in range(R):
        line = tvar[:, r * tree : (r + 1) * tree]
        hot = jnp.where(trow < TERMS * NVAR, (line == trow % NVAR).astype(f32), 0.0).astype(bf16)
        tvoh[r] = hot
        matched = dot(hot, spread) > 0.5
        terms = jnp.where(matched, same_terms, other_terms)
        bmat[r] = jnp.where(brow == TERMS * NVAR, low, terms).astype(bf16)

    up = parents[...]
    eye = (iota((tree, tree), 0) == iota((tree, tree), 1)).astype(f32)
    reach = ((iota((tree, tree), 0) == up).astype(f32) + eye).astype(bf16)
    clip = lambda v: jnp.minimum(v, 1.0).astype(bf16)
    reach2 = clip(dot(reach, reach))
    reach4 = clip(dot(reach2, reach2))
    reach8 = clip(dot(reach4, reach4))
    allowed = dot(reach8, spread) > 0.5

    block = (iota((C, QL), 0) // tree == iota((C, QL), 1) // HD).astype(f32).astype(bf16)

    def spread_query(q):
        return jnp.concatenate([q] * HL, axis=0) * block

    head_lanes = iota((HD, C), 1) // tree

    def pick(wide):
        out = wide[0:HD]
        for h in range(1, HL):
            out = jnp.where(head_lanes == h, wide[h * HD : (h + 1) * HD], out)
        return out

    tree_scores = dot(keys, spread_query(query), 1, 1) + dot(tvoh[req], bmat[req], 0, 0)
    tree_max = jnp.max(jnp.where(allowed, tree_scores, low), axis=0, keepdims=True)
    tree_w = jnp.where(allowed, jnp.exp(tree_scores - tree_max), 0.0).astype(bf16)
    tree_total = jnp.sum(tree_w.astype(f32), axis=0, keepdims=True)
    tree_out = pick(dot(vals, tree_w, 0, 0))

    get_pages.wait()

    @pl.loop(0, pool // group)
    def _(g):
        for k in range(group):
            vt[g * group + k] = pages[1, g * group + k].T

    @pl.loop(0, half)
    def _(k):
        forward_copy(k).wait()

    @pl.loop(0, pool // group)
    def _(g):
        for k in range(group):
            p = g * group + k
            owner = own_s[p]
            scores = dot(pages[0, p], spread_query(qbuf[owner]), 1, 1) + dot(oh[p], bmat[owner], 0, 0)
            top = jnp.max(scores, axis=0, keepdims=True)
            w = jnp.exp(scores - top).astype(bf16)
            pm[pl.ds(p, 1), :] = top
            plt[pl.ds(p, 1), :] = jnp.sum(w.astype(f32), axis=0, keepdims=True)
            po[p] = pick(dot(vt[p], w))

    def out_copy(d):
        return remote(osend.at[d], obuf.at[d], os_.at[d], or_.at[d], at_req(d))

    def stat_copy(d):
        return remote(ssend.at[d], sbuf.at[d], ss.at[d], sr.at[d], at_req(d))

    def merged(r):
        mask = own_rows[...] == r
        maxes = pm[...]
        top = jnp.max(jnp.where(mask, maxes, low), axis=0, keepdims=True)
        factor = jnp.where(mask, jnp.exp(maxes - top), 0.0)
        total = jnp.sum(factor * plt[...], axis=0, keepdims=True)
        out = factor[0:1] * po[0]
        for p in range(1, pool):
            out = out + factor[p : p + 1] * po[p]
        return top, total, out

    @pl.loop(1, R)
    def _(d):
        top, total, out = merged(lax.rem(req + d, R))
        osend[d] = out.astype(bf16)
        ssend[d] = jnp.concatenate([top, total], axis=0)
        out_copy(d).start()
        stat_copy(d).start()

    top, total, out = merged(req)
    new_top = jnp.maximum(top, tree_max)
    fa = jnp.exp(top - new_top)
    fb = jnp.exp(tree_max - new_top)
    total = total * fa + tree_total * fb
    out = out * fa + tree_out * fb
    top = new_top

    @pl.loop(1, R)
    def _(d):
        out_copy(d).wait()
        stat_copy(d).wait()

    final_top = top
    for d in range(1, R):
        final_top = jnp.maximum(final_top, sbuf[d][0:1])
    fa = jnp.exp(top - final_top)
    total = total * fa
    out = out * fa
    for d in range(1, R):
        stats = sbuf[d]
        fd = jnp.exp(stats[0:1] - final_top)
        total = total + stats[1:2] * fd
        out = out + obuf[d].astype(f32) * fd
    att_t = (out / total).astype(bf16)
    diag = jnp.concatenate([att_t] * HL, axis=0) * (
        iota((HL * HD, C), 0) // HD == iota((HL * HD, C), 1) // tree
    ).astype(f32).astype(bf16)
    att = dot(spread, diag, 1, 1).astype(bf16)
    gbuf[head] = att
    att_copies = [remote(gbuf.at[head], gbuf.at[head], gs.at[d - 1], gr.at[d - 1], at_head(d)) for d in range(1, H)]
    for copy in att_copies:
        copy.start()
    attended[...] = att
    get_out.wait()
    state = values + dot(att, outw[pl.ds(pl.multiple_of(head * QL, QL), QL), :])
    for d in range(1, H):
        att_copies[d - 1].wait()
        source = lax.rem(head + H - d, H)
        state = state + dot(gbuf[source], outw[pl.ds(pl.multiple_of(source * QL, QL), QL), :])
    state = state.astype(bf16).astype(f32)
    hid[...] = state.reshape(H, rows, D)
    normed_two = rms_scaled(state, gains[1:2, :]).astype(bf16)
    get_gu.wait()
    step = STEP
    for c in range(0, FFL, step):
        gate = dot(normed_two, gu[0, :, c : c + step])
        upward = dot(normed_two, gu[1, :, c : c + step])
        act[:, c : c + step] = (gate / (1.0 + jnp.exp(-gate)) * upward).astype(bf16)
    get_down.wait()
    activated = act[...]
    def down_copy(d, n):
        columns = pl.ds(n * step, step)
        return remote(
            dsend.at[lax.rem(head + d, H), :, columns], dbuf.at[d - 1, :, columns],
            ds_.at[d - 1, n], dr.at[d - 1, n], at_head(d),
        )

    for n in range(D // step):
        part = dot(activated, downw[:, n * step : (n + 1) * step])
        dsend[:, :, n * step : (n + 1) * step] = part.reshape(H, rows, step).astype(bf16)
        for d in range(1, H):
            down_copy(d, n).start()
    result = dsend[head].astype(f32)
    for d in range(1, H):
        for n in range(D // step):
            down_copy(d, n).wait()
        result = result + dbuf[d - 1].astype(f32)
    mixed[...] = (hid[head] + result).astype(bf16)


def hand_over(mixed, attended, new_kv, mixed_out, attended_out, new_kv_out, one, two, three, sem):
    fetch = [
        pltpu.make_async_copy(src, dst, sem.at[k])
        for k, (src, dst) in enumerate(((mixed, one), (attended, two), (new_kv, three)))
    ]
    store = [
        pltpu.make_async_copy(src, dst, sem.at[3 + k])
        for k, (src, dst) in enumerate(((one, mixed_out), (two, attended_out), (three, new_kv_out)))
    ]
    for copy in fetch:
        copy.start()
    for k in range(3):
        fetch[k].wait()
        store[k].start()
    for copy in store:
        copy.wait()


def shards(
    tokens, gains, qkv_weight, out_weight, gate_up_weight, down_weight, variate_bias, page_cache, page_variates,
    token_variates, cache_len, page_table, parents, accepted,
):
    R = lax.axis_size("req")
    H = lax.axis_size("head")
    rows, D = tokens.shape
    QL = qkv_weight.shape[2]
    HL = QL // HD
    pool, page = page_variates.shape
    tree = parents.shape[1]
    C = HL * tree
    padded = (pool + 7) // 8 * 8
    hbm = pl.BlockSpec(memory_space=pl.ANY)
    vmem = pl.BlockSpec(memory_space=pltpu.VMEM)
    dma = pltpu.SemaphoreType.DMA
    results = pl.pallas_call(
        functools.partial(kernel, R, H),
        out_shape=(
            jax.ShapeDtypeStruct((rows, D), bf16),
            jax.ShapeDtypeStruct((tree, QL), bf16),
            jax.ShapeDtypeStruct((2, 1, accepted.shape[1], QL), bf16),
        ),
        in_specs=[hbm] * 14,
        out_specs=(vmem, vmem, vmem),
        scratch_shapes=[
            pltpu.VMEM(gains.shape, f32),
            pltpu.SMEM(variate_bias.shape, f32),
            pltpu.VMEM(page_variates.shape, jnp.int32),
            pltpu.VMEM((1, token_variates.shape[0]), jnp.int32),
            pltpu.SMEM(cache_len.shape, jnp.int32),
            pltpu.VMEM(page_table.shape, jnp.int32),
            pltpu.VMEM(parents.shape, jnp.int32),
            pltpu.VMEM(accepted.shape, jnp.int32),
            pltpu.VMEM((pool, QL, page), bf16),
            pltpu.VMEM(qkv_weight.shape, bf16),
            pltpu.VMEM(out_weight.shape, bf16),
            pltpu.VMEM(gate_up_weight.shape, bf16),
            pltpu.VMEM(down_weight.shape, bf16),
            pltpu.VMEM(page_cache.shape, bf16),
            pltpu.VMEM((H, rows, D), bf16),
            pltpu.VMEM((R, tree, QL), bf16),
            pltpu.VMEM((R, BROWS, tree), bf16),
            pltpu.VMEM((R, BROWS, C), bf16),
            pltpu.VMEM((pool, BROWS, page), bf16),
            pltpu.SMEM((pool,), jnp.int32),
            pltpu.VMEM((padded, C), jnp.int32),
            pltpu.VMEM((padded, C), f32),
            pltpu.VMEM((padded, C), f32),
            pltpu.VMEM((pool, HD, C), f32),
            pltpu.VMEM((R, HD, C), bf16),
            pltpu.VMEM((R, 2, C), f32),
            pltpu.VMEM((R, HD, C), bf16),
            pltpu.VMEM((R, 2, C), f32),
            pltpu.VMEM((H, tree, QL), bf16),
            pltpu.VMEM((tree, gate_up_weight.shape[2]), bf16),
            pltpu.VMEM((H, rows, D), f32),
            pltpu.VMEM((H, rows, D), bf16),
            pltpu.VMEM((H, rows, D), bf16),
            dma((6,)),
            dma((8,)),
            dma((H,)), dma((H,)),
            dma((R,)), dma((R,)),
            dma((R,)), dma((R,)),
            dma((R,)), dma((R,)),
            dma((R,)), dma((R,)),
            dma((H,)), dma((H,)),
            dma((H, D // STEP)), dma((H, D // STEP)),
        ],
        compiler_params=pltpu.CompilerParams(
            collective_id=0, has_side_effects=True, vmem_limit_bytes=60 * 1024 * 1024
        ),
        cost_estimate=pl.CostEstimate(flops=10**9, bytes_accessed=12 * 10**6, transcendentals=10**6),
    )(
        tokens, gains, qkv_weight, out_weight, gate_up_weight, down_weight, variate_bias, page_cache, page_variates,
        token_variates.reshape(1, -1), cache_len, page_table, parents, accepted,
    )
    return tuple(pl.pallas_call(
        hand_over,
        out_shape=tuple(jax.ShapeDtypeStruct(a.shape, a.dtype) for a in results),
        in_specs=[hbm] * 3,
        out_specs=(hbm,) * 3,
        scratch_shapes=[pltpu.VMEM(a.shape, a.dtype) for a in results] + [dma((6,))],
        compiler_params=pltpu.CompilerParams(vmem_limit_bytes=60 * 1024 * 1024),
    )(*results))


def solution(mesh):
    return jax.shard_map(
        shards,
        mesh=mesh,
        in_specs=(
            P(("req", "head"), None),
            P(),
            P(None, None, "head"),
            P(),
            P(None, None, "head"),
            P("head", None),
            P(),
            P(None, "req", None, "head"),
            P("req", None),
            P(),
            P(),
            P(),
            P("req", None),
            P("req", None),
        ),
        out_specs=(P(("req", "head"), None), P("req", "head"), P(None, "req", None, "head")),
        check_vma=False,
    )
```

```python
import functools
import math

import jax
import jax.numpy as jnp
from jax import lax
from jax.experimental import pallas as pl
from jax.experimental.pallas import tpu as pltpu
from jax.sharding import PartitionSpec as P

HD = 64
NVAR = 4
TERMS = 3
BROWS = 16
STEP = 256
epsilon = 1e-06
low = -1e30
f32 = jnp.float32
bf16 = jnp.bfloat16


def rms_scaled(values, gain):
    return values * lax.rsqrt(jnp.mean(values * values, axis=-1, keepdims=True) + epsilon) * gain


def iota(shape, dim):
    return lax.broadcasted_iota(jnp.int32, shape, dim)


def dot(a, b, ca=1, cb=0):
    return lax.dot_general(a, b, (((ca,), (cb,)), ((), ())), preferred_element_type=f32)


def kernel(
    R, H,
    tokens, gains_hbm, qkv_hbm, out_hbm, gu_hbm, down_hbm, vbias_hbm, cache_hbm, pvar_hbm, tvar_hbm, clen_hbm,
    ptab_hbm, parents_hbm, accepted_hbm,
    mixed, attended, new_kv,
    gains, vbias, pvar, tvar, clen, ptab, parents, accepted, vt, oht,
    qkv, outw, gu, downw, pages, tbuf, qbuf, tvoh, bmat, oh, own_s, own_rows, pm, plt, po,
    osend, ssend, obuf, sbuf, gbuf, act, hid, dsend, dbuf,
    lsem, ksem, ts, tr, qs, qr, fs, fr, os_, or_, ss, sr, gs, gr, ds_, dr,
):
    req = lax.axis_index("req")
    head = lax.axis_index("head")
    rows, D = tokens.shape
    QL = qkv.shape[2]
    HL = QL // HD
    pool, page = pvar.shape
    maxp = ptab.shape[1]
    tree = parents.shape[1]
    C = HL * tree
    FFL = gu.shape[2]

    def at_head(d):
        return {"req": req, "head": lax.rem(head + d, H)}

    def at_req(d):
        return {"req": lax.rem(req + d, R), "head": head}

    def remote(src, dst, s, r, device):
        return pltpu.make_async_remote_copy(
            src_ref=src, dst_ref=dst, send_sem=s, recv_sem=r, device_id=device, device_id_type=pl.DeviceIdType.MESH
        )

    barrier = pltpu.get_barrier_semaphore()
    for d in range(1, H):
        pl.semaphore_signal(barrier, inc=1, device_id=at_head(d), device_id_type=pl.DeviceIdType.MESH)

    @pl.loop(1, R)
    def _(d):
        pl.semaphore_signal(barrier, inc=1, device_id=at_req(d), device_id_type=pl.DeviceIdType.MESH)

    small = [
        pltpu.make_async_copy(src, dst, ksem.at[k])
        for k, (src, dst) in enumerate((
            (ptab_hbm, ptab), (pvar_hbm, pvar), (clen_hbm, clen), (tvar_hbm, tvar), (vbias_hbm, vbias),
            (parents_hbm, parents), (accepted_hbm, accepted), (gains_hbm, gains),
        ))
    ]
    for copy in small:
        copy.start()
    own_tokens = pltpu.make_async_copy(tokens, tbuf.at[head], lsem.at[0])
    own_tokens.start()
    get_qkv = pltpu.make_async_copy(qkv_hbm, qkv, lsem.at[1])
    get_qkv.start()
    get_pages = pltpu.make_async_copy(cache_hbm, pages, lsem.at[2])
    get_pages.start()
    get_out = pltpu.make_async_copy(out_hbm, outw, lsem.at[3])
    get_gu = pltpu.make_async_copy(gu_hbm, gu, lsem.at[4])
    get_down = pltpu.make_async_copy(down_hbm, downw, lsem.at[5])
    get_out.start()
    get_gu.start()
    get_down.start()
    pl.semaphore_wait(barrier, H - 1 + R - 1)

    token_copies = [
        remote(tokens, tbuf.at[head], ts.at[d - 1], tr.at[d - 1], at_head(d)) for d in range(1, H)
    ]
    for copy in token_copies:
        copy.start()

    for copy in small:
        copy.wait()
    table = ptab[...]
    place = iota(table.shape, 0) * maxp + iota(table.shape, 1) + 1
    row16 = iota((BROWS, page), 0)
    lane16 = iota((BROWS, page), 1)
    own_rows[...] = jnp.full(own_rows.shape, -1, jnp.int32)
    pm[...] = jnp.zeros(pm.shape, f32)
    plt[...] = jnp.zeros(plt.shape, f32)

    group = 4 if pool % 4 == 0 else 1

    @pl.loop(0, pool // group)
    def _(g):
        for k in range(group):
            p = g * group + k
            code = jnp.max(jnp.where(table == req * pool + p, place, 0))
            used = code > 0
            slot = jnp.maximum(code - 1, 0)
            owner = slot // maxp
            filled = jnp.where(used, jnp.clip(clen[owner] - (slot - owner * maxp) * page, 0, page), 0)
            own_s[p] = owner
            own_rows[pl.ds(p, 1), :] = jnp.full((1, C), jnp.where(used, owner, -1), jnp.int32)
            line = pvar[pl.ds(p, 1), :]
            hot = jnp.where(row16 < TERMS * NVAR, (line == row16 % NVAR).astype(f32), 0.0)
            hot = jnp.where(row16 == TERMS * NVAR, (lane16 >= filled).astype(f32), hot)
            oh[p] = hot.astype(bf16)

    spread = (iota((tree, C), 0) == iota((tree, C), 1) % tree).astype(f32).astype(bf16)
    block = (iota((QL, C), 0) // HD == iota((QL, C), 1) // tree).astype(f32).astype(bf16)
    head_lanes = iota((HD, C), 1) // tree

    def pick(wide):
        out = wide[0:HD]
        for h in range(1, HL):
            out = jnp.where(head_lanes == h, wide[h * HD : (h + 1) * HD], out)
        return out

    own_tokens.wait()
    for copy in token_copies:
        copy.wait()
    get_qkv.wait()
    values = tbuf[...].astype(f32).reshape(H * rows, D)
    normed = rms_scaled(values, gains[0:1, :]).astype(bf16)
    scale = 1.0 / math.sqrt(HD)
    query = (dot(normed, qkv[0]).astype(bf16).astype(f32) * scale).astype(bf16)
    query = pick(dot(query, spread, 0, 0)).astype(bf16)
    qbuf[req] = query

    half = R // 2
    partner = req + 1 - 2 * lax.rem(req, 2)
    beside = {"req": partner, "head": head}

    def query_copy(k):
        return remote(qbuf.at[req], qbuf.at[req], qs.at[k], qr.at[k], at_req(2 * k))

    def forward_copy(k):
        source = lax.rem(req + R - 2 * k, R)
        return remote(qbuf.at[source], qbuf.at[source], fs.at[k], fr.at[k], beside)

    @pl.loop(1, half)
    def _(k):
        query_copy(k).start()

    forward_copy(0).start()

    keys = dot(normed, qkv[1]).astype(bf16)
    vals = dot(normed, qkv[2]).astype(bf16)
    chosen = (iota((tree, accepted.shape[1]), 0) == accepted[...]).astype(f32).astype(bf16)
    new_kv[0, 0] = dot(chosen, keys, 0, 0).astype(bf16)
    new_kv[1, 0] = dot(chosen, vals, 0, 0).astype(bf16)

    @pl.loop(1, half)
    def _(k):
        query_copy(k).wait()
        forward_copy(k).start()

    lane_head = iota((1, C), 1) // tree
    same_row = jnp.zeros((1, C), f32)
    other_row = jnp.zeros((1, C), f32)
    for h in range(HL):
        same_row = jnp.where(lane_head == h, vbias[0, head * HL + h], same_row)
        other_row = jnp.where(lane_head == h, vbias[1, head * HL + h], other_row)

    def split(row):
        one = row.astype(bf16).astype(f32)
        two = (row - one).astype(bf16).astype(f32)
        three = (row - one - two).astype(bf16).astype(f32)
        term = iota((BROWS, C), 0) // NVAR
        return jnp.where(term == 0, one, jnp.where(term == 1, two, jnp.where(term == 2, three, 0.0)))

    same_terms = split(same_row)
    other_terms = split(other_row)
    brow = iota((BROWS, C), 0)
    trow = iota((BROWS, tree), 0)
    for r in range(R):
        line = tvar[:, r * tree : (r + 1) * tree]
        hot = jnp.where(trow < TERMS * NVAR, (line == trow % NVAR).astype(f32), 0.0).astype(bf16)
        tvoh[r] = hot
        matched = dot(hot, spread) > 0.5
        terms = jnp.where(matched, same_terms, other_terms)
        bmat[r] = jnp.where(brow == TERMS * NVAR, low, terms).astype(bf16)

    up = parents[...]
    eye = (iota((tree, tree), 0) == iota((tree, tree), 1)).astype(f32)
    reach = ((iota((tree, tree), 0) == up).astype(f32) + eye).astype(bf16)
    clip = lambda v: jnp.minimum(v, 1.0).astype(bf16)
    reach2 = clip(dot(reach, reach))
    reach4 = clip(dot(reach2, reach2))
    reach8 = clip(dot(reach4, reach4))
    allowed = dot(reach8, spread) > 0.5

    def spread_query(q):
        return jnp.concatenate([q] * HL, axis=0) * block

    tree_scores = dot(keys, spread_query(query)) + dot(tvoh[req], bmat[req], 0, 0)
    tree_max = jnp.max(jnp.where(allowed, tree_scores, low), axis=0, keepdims=True)
    tree_w = jnp.where(allowed, jnp.exp(tree_scores - tree_max), 0.0).astype(bf16)
    tree_total = jnp.sum(tree_w.astype(f32), axis=0, keepdims=True)
    tree_out = pick(dot(vals, tree_w, 0, 0))

    get_pages.wait()

    @pl.loop(0, pool // group)
    def _(g):
        for k in range(group):
            vt[g * group + k] = pages[1, g * group + k].T
            oht[g * group + k] = oh[g * group + k].T

    @pl.loop(0, half)
    def _(k):
        forward_copy(k).wait()

    @pl.loop(0, pool // group)
    def _(g):
        for k in range(group):
            p = g * group + k
            owner = own_s[p]
            scores = dot(pages[0, p], spread_query(qbuf[owner])) + dot(oht[p], bmat[owner])
            top = jnp.max(scores, axis=0, keepdims=True)
            w = jnp.exp(scores - top).astype(bf16)
            pm[pl.ds(p, 1), :] = top
            plt[pl.ds(p, 1), :] = jnp.sum(w.astype(f32), axis=0, keepdims=True)
            po[p] = pick(dot(vt[p], w))

    def out_copy(d):
        return remote(osend.at[d], obuf.at[d], os_.at[d], or_.at[d], at_req(d))

    def stat_copy(d):
        return remote(ssend.at[d], sbuf.at[d], ss.at[d], sr.at[d], at_req(d))

    def merged(r):
        mask = own_rows[...] == r
        maxes = pm[...]
        top = jnp.max(jnp.where(mask, maxes, low), axis=0, keepdims=True)
        factor = jnp.where(mask, jnp.exp(maxes - top), 0.0)
        total = jnp.sum(factor * plt[...], axis=0, keepdims=True)
        out = factor[0:1] * po[0]
        for p in range(1, pool):
            out = out + factor[p : p + 1] * po[p]
        return top, total, out

    @pl.loop(1, R)
    def _(d):
        top, total, out = merged(lax.rem(req + d, R))
        osend[d] = out.astype(bf16)
        ssend[d] = jnp.concatenate([top, total], axis=0)
        out_copy(d).start()
        stat_copy(d).start()

    top, total, out = merged(req)
    new_top = jnp.maximum(top, tree_max)
    fa = jnp.exp(top - new_top)
    fb = jnp.exp(tree_max - new_top)
    total = total * fa + tree_total * fb
    out = out * fa + tree_out * fb
    top = new_top

    @pl.loop(1, R)
    def _(d):
        out_copy(d).wait()
        stat_copy(d).wait()

    final_top = top
    for d in range(1, R):
        final_top = jnp.maximum(final_top, sbuf[d][0:1])
    fa = jnp.exp(top - final_top)
    total = total * fa
    out = out * fa
    for d in range(1, R):
        stats = sbuf[d]
        fd = jnp.exp(stats[0:1] - final_top)
        total = total + stats[1:2] * fd
        out = out + obuf[d].astype(f32) * fd
    att_t = (out / total).astype(bf16)
    att = dot(spread, spread_query(att_t), 1, 1).astype(bf16)
    gbuf[head] = att
    att_copies = [remote(gbuf.at[head], gbuf.at[head], gs.at[d - 1], gr.at[d - 1], at_head(d)) for d in range(1, H)]
    for copy in att_copies:
        copy.start()
    attended[...] = att
    get_out.wait()
    state = values + dot(att, outw[pl.ds(pl.multiple_of(head * QL, QL), QL), :])
    for d in range(1, H):
        att_copies[d - 1].wait()
        source = lax.rem(head + H - d, H)
        state = state + dot(gbuf[source], outw[pl.ds(pl.multiple_of(source * QL, QL), QL), :])
    state = state.astype(bf16).astype(f32)
    hid[...] = state.reshape(H, rows, D)
    normed_two = rms_scaled(state, gains[1:2, :]).astype(bf16)
    get_gu.wait()
    step = STEP
    for c in range(0, FFL, step):
        gate = dot(normed_two, gu[0, :, c : c + step])
        upward = dot(normed_two, gu[1, :, c : c + step])
        act[:, c : c + step] = (gate / (1.0 + jnp.exp(-gate)) * upward).astype(bf16)
    get_down.wait()
    activated = act[...]
    def down_copy(d, n):
        columns = pl.ds(n * step, step)
        return remote(
            dsend.at[lax.rem(head + d, H), :, columns], dbuf.at[d - 1, :, columns],
            ds_.at[d - 1, n], dr.at[d - 1, n], at_head(d),
        )

    for n in range(D // step):
        part = dot(activated, downw[:, n * step : (n + 1) * step])
        dsend[:, :, n * step : (n + 1) * step] = part.reshape(H, rows, step).astype(bf16)
        for d in range(1, H):
            down_copy(d, n).start()
    result = dsend[head].astype(f32)
    for d in range(1, H):
        for n in range(D // step):
            down_copy(d, n).wait()
        result = result + dbuf[d - 1].astype(f32)
    mixed[...] = (hid[head] + result).astype(bf16)


def hand_over(mixed, attended, new_kv, mixed_out, attended_out, new_kv_out, one, two, three, sem):
    fetch = [
        pltpu.make_async_copy(src, dst, sem.at[k])
        for k, (src, dst) in enumerate(((mixed, one), (attended, two), (new_kv, three)))
    ]
    store = [
        pltpu.make_async_copy(src, dst, sem.at[3 + k])
        for k, (src, dst) in enumerate(((one, mixed_out), (two, attended_out), (three, new_kv_out)))
    ]
    for copy in fetch:
        copy.start()
    for k in range(3):
        fetch[k].wait()
        store[k].start()
    for copy in store:
        copy.wait()


def shards(
    tokens, gains, qkv_weight, out_weight, gate_up_weight, down_weight, variate_bias, page_cache, page_variates,
    token_variates, cache_len, page_table, parents, accepted,
):
    R = lax.axis_size("req")
    H = lax.axis_size("head")
    rows, D = tokens.shape
    QL = qkv_weight.shape[2]
    HL = QL // HD
    pool, page = page_variates.shape
    tree = parents.shape[1]
    C = HL * tree
    padded = (pool + 7) // 8 * 8
    hbm = pl.BlockSpec(memory_space=pl.ANY)
    vmem = pl.BlockSpec(memory_space=pltpu.VMEM)
    dma = pltpu.SemaphoreType.DMA
    results = pl.pallas_call(
        functools.partial(kernel, R, H),
        out_shape=(
            jax.ShapeDtypeStruct((rows, D), bf16),
            jax.ShapeDtypeStruct((tree, QL), bf16),
            jax.ShapeDtypeStruct((2, 1, accepted.shape[1], QL), bf16),
        ),
        in_specs=[hbm] * 14,
        out_specs=(vmem, vmem, vmem),
        scratch_shapes=[
            pltpu.VMEM(gains.shape, f32),
            pltpu.SMEM(variate_bias.shape, f32),
            pltpu.VMEM(page_variates.shape, jnp.int32),
            pltpu.VMEM((1, token_variates.shape[0]), jnp.int32),
            pltpu.SMEM(cache_len.shape, jnp.int32),
            pltpu.VMEM(page_table.shape, jnp.int32),
            pltpu.VMEM(parents.shape, jnp.int32),
            pltpu.VMEM(accepted.shape, jnp.int32),
            pltpu.VMEM((pool, QL, page), bf16),
            pltpu.VMEM((pool, page, BROWS), bf16),
            pltpu.VMEM(qkv_weight.shape, bf16),
            pltpu.VMEM(out_weight.shape, bf16),
            pltpu.VMEM(gate_up_weight.shape, bf16),
            pltpu.VMEM(down_weight.shape, bf16),
            pltpu.VMEM(page_cache.shape, bf16),
            pltpu.VMEM((H, rows, D), bf16),
            pltpu.VMEM((R, HD, C), bf16),
            pltpu.VMEM((R, BROWS, tree), bf16),
            pltpu.VMEM((R, BROWS, C), bf16),
            pltpu.VMEM((pool, BROWS, page), bf16),
            pltpu.SMEM((pool,), jnp.int32),
            pltpu.VMEM((padded, C), jnp.int32),
            pltpu.VMEM((padded, C), f32),
            pltpu.VMEM((padded, C), f32),
            pltpu.VMEM((pool, HD, C), f32),
            pltpu.VMEM((R, HD, C), bf16),
            pltpu.VMEM((R, 2, C), f32),
            pltpu.VMEM((R, HD, C), bf16),
            pltpu.VMEM((R, 2, C), f32),
            pltpu.VMEM((H, tree, QL), bf16),
            pltpu.VMEM((tree, gate_up_weight.shape[2]), bf16),
            pltpu.VMEM((H, rows, D), f32),
            pltpu.VMEM((H, rows, D), bf16),
            pltpu.VMEM((H, rows, D), bf16),
            dma((6,)),
            dma((8,)),
            dma((H,)), dma((H,)),
            dma((R,)), dma((R,)),
            dma((R,)), dma((R,)),
            dma((R,)), dma((R,)),
            dma((R,)), dma((R,)),
            dma((H,)), dma((H,)),
            dma((H, D // STEP)), dma((H, D // STEP)),
        ],
        compiler_params=pltpu.CompilerParams(
            collective_id=0, has_side_effects=True, vmem_limit_bytes=60 * 1024 * 1024
        ),
        cost_estimate=pl.CostEstimate(flops=10**9, bytes_accessed=12 * 10**6, transcendentals=10**6),
    )(
        tokens, gains, qkv_weight, out_weight, gate_up_weight, down_weight, variate_bias, page_cache, page_variates,
        token_variates.reshape(1, -1), cache_len, page_table, parents, accepted,
    )
    return tuple(pl.pallas_call(
        hand_over,
        out_shape=tuple(jax.ShapeDtypeStruct(a.shape, a.dtype) for a in results),
        in_specs=[hbm] * 3,
        out_specs=(hbm,) * 3,
        scratch_shapes=[pltpu.VMEM(a.shape, a.dtype) for a in results] + [dma((6,))],
        compiler_params=pltpu.CompilerParams(vmem_limit_bytes=60 * 1024 * 1024),
    )(*results))


def solution(mesh):
    return jax.shard_map(
        shards,
        mesh=mesh,
        in_specs=(
            P(("req", "head"), None),
            P(),
            P(None, None, "head"),
            P(),
            P(None, None, "head"),
            P("head", None),
            P(),
            P(None, "req", None, "head"),
            P("req", None),
            P(),
            P(),
            P(),
            P("req", None),
            P("req", None),
        ),
        out_specs=(P(("req", "head"), None), P("req", "head"), P(None, "req", None, "head")),
        check_vma=False,
    )
```

```python
import functools
import math

import jax
import jax.numpy as jnp
from jax import lax
from jax.experimental import pallas as pl
from jax.experimental.pallas import tpu as pltpu
from jax.sharding import PartitionSpec as P

HD = 64
NVAR = 4
TERMS = 3
BROWS = 16
STEP = 256
epsilon = 1e-06
low = -1e30
f32 = jnp.float32
bf16 = jnp.bfloat16


def rms_scaled(values, gain):
    return values * lax.rsqrt(jnp.mean(values * values, axis=-1, keepdims=True) + epsilon) * gain


def iota(shape, dim):
    return lax.broadcasted_iota(jnp.int32, shape, dim)


def dot(a, b, ca=1, cb=0):
    return lax.dot_general(a, b, (((ca,), (cb,)), ((), ())), preferred_element_type=f32)


def kernel(
    R, H,
    tokens, gains_hbm, qkv_hbm, out_hbm, gu_hbm, down_hbm, vbias_hbm, cache_hbm, pvar_hbm, tvar_hbm, clen_hbm,
    ptab_hbm, parents_hbm, accepted_hbm,
    mixed, attended, new_kv,
    gains, vbias, pvar, tvar, clen, ptab, parents, accepted, vt, oht,
    qkv, outw, gu, downw, pages, tbuf, qbuf, tvoh, bmat, oh, own_s, own_rows, pm, plt, po,
    osend, ssend, obuf, sbuf, gbuf, act, hid, dsend, dbuf,
    lsem, ksem, ts, tr, qs, qr, fs, fr, os_, or_, ss, sr, gs, gr, ds_, dr,
):
    req = lax.axis_index("req")
    head = lax.axis_index("head")
    rows, D = tokens.shape
    QL = qkv.shape[2]
    HL = QL // HD
    pool, page = pvar.shape
    maxp = ptab.shape[1]
    tree = parents.shape[1]
    C = HL * tree
    FFL = gu.shape[2]

    def at_head(d):
        return {"req": req, "head": lax.rem(head + d, H)}

    def at_req(d):
        return {"req": lax.rem(req + d, R), "head": head}

    def remote(src, dst, s, r, device):
        return pltpu.make_async_remote_copy(
            src_ref=src, dst_ref=dst, send_sem=s, recv_sem=r, device_id=device, device_id_type=pl.DeviceIdType.MESH
        )

    barrier = pltpu.get_barrier_semaphore()
    for d in range(1, H):
        pl.semaphore_signal(barrier, inc=1, device_id=at_head(d), device_id_type=pl.DeviceIdType.MESH)

    @pl.loop(1, R)
    def _(d):
        pl.semaphore_signal(barrier, inc=1, device_id=at_req(d), device_id_type=pl.DeviceIdType.MESH)

    small = [
        pltpu.make_async_copy(src, dst, ksem.at[k])
        for k, (src, dst) in enumerate((
            (ptab_hbm, ptab), (pvar_hbm, pvar), (clen_hbm, clen), (tvar_hbm, tvar), (vbias_hbm, vbias),
            (parents_hbm, parents), (accepted_hbm, accepted), (gains_hbm, gains),
        ))
    ]
    for copy in small:
        copy.start()
    own_tokens = pltpu.make_async_copy(tokens, tbuf.at[head], lsem.at[0])
    own_tokens.start()
    get_qkv = pltpu.make_async_copy(qkv_hbm, qkv, lsem.at[1])
    get_qkv.start()
    get_pages = pltpu.make_async_copy(cache_hbm, pages, lsem.at[2])
    get_pages.start()
    get_out = pltpu.make_async_copy(out_hbm, outw, lsem.at[3])
    get_gu = pltpu.make_async_copy(gu_hbm, gu, lsem.at[4])
    get_down = pltpu.make_async_copy(down_hbm, downw, lsem.at[5])
    get_out.start()
    get_gu.start()
    get_down.start()
    pl.semaphore_wait(barrier, H - 1 + R - 1)

    token_copies = [
        remote(tokens, tbuf.at[head], ts.at[d - 1], tr.at[d - 1], at_head(d)) for d in range(1, H)
    ]
    for copy in token_copies:
        copy.start()

    for copy in small:
        copy.wait()
    table = ptab[...]
    place = iota(table.shape, 0) * maxp + iota(table.shape, 1) + 1
    row16 = iota((BROWS, page), 0)
    lane16 = iota((BROWS, page), 1)
    own_rows[...] = jnp.full(own_rows.shape, -1, jnp.int32)
    pm[...] = jnp.zeros(pm.shape, f32)
    plt[...] = jnp.zeros(plt.shape, f32)

    group = 4 if pool % 4 == 0 else 1

    @pl.loop(0, pool // group)
    def _(g):
        for k in range(group):
            p = g * group + k
            code = jnp.max(jnp.where(table == req * pool + p, place, 0))
            used = code > 0
            slot = jnp.maximum(code - 1, 0)
            owner = slot // maxp
            filled = jnp.where(used, jnp.clip(clen[owner] - (slot - owner * maxp) * page, 0, page), 0)
            own_s[p] = owner
            own_rows[pl.ds(p, 1), :] = jnp.full((1, C), jnp.where(used, owner, -1), jnp.int32)
            line = pvar[pl.ds(p, 1), :]
            hot = jnp.where(row16 < TERMS * NVAR, (line == row16 % NVAR).astype(f32), 0.0)
            hot = jnp.where(row16 == TERMS * NVAR, (lane16 >= filled).astype(f32), hot)
            oh[p] = hot.astype(bf16)

    spread = (iota((tree, C), 0) == iota((tree, C), 1) % tree).astype(f32).astype(bf16)
    block = (iota((QL, C), 0) // HD == iota((QL, C), 1) // tree).astype(f32).astype(bf16)
    head_lanes = iota((HD, C), 1) // tree

    def pick(wide):
        out = wide[0:HD]
        for h in range(1, HL):
            out = jnp.where(head_lanes == h, wide[h * HD : (h + 1) * HD], out)
        return out

    own_tokens.wait()
    for copy in token_copies:
        copy.wait()
    get_qkv.wait()
    values = tbuf[...].astype(f32).reshape(H * rows, D)
    normed = rms_scaled(values, gains[0:1, :]).astype(bf16)
    scale = 1.0 / math.sqrt(HD)
    query = (dot(normed, qkv[0]).astype(bf16).astype(f32) * scale).astype(bf16)
    query = pick(dot(query, spread, 0, 0)).astype(bf16)
    qbuf[req] = query

    half = R // 2
    partner = req + 1 - 2 * lax.rem(req, 2)
    beside = {"req": partner, "head": head}

    def query_copy(k):
        return remote(qbuf.at[req], qbuf.at[req], qs.at[k], qr.at[k], at_req(2 * k))

    def forward_copy(k):
        source = lax.rem(req + R - 2 * k, R)
        return remote(qbuf.at[source], qbuf.at[source], fs.at[k], fr.at[k], beside)

    @pl.loop(1, half)
    def _(k):
        query_copy(k).start()

    forward_copy(0).start()

    keys = dot(normed, qkv[1]).astype(bf16)
    vals = dot(normed, qkv[2]).astype(bf16)
    chosen = (iota((tree, accepted.shape[1]), 0) == accepted[...]).astype(f32).astype(bf16)
    new_kv[0, 0] = dot(chosen, keys, 0, 0).astype(bf16)
    new_kv[1, 0] = dot(chosen, vals, 0, 0).astype(bf16)

    @pl.loop(1, half)
    def _(k):
        query_copy(k).wait()
        forward_copy(k).start()

    lane_head = iota((1, C), 1) // tree
    same_row = jnp.zeros((1, C), f32)
    other_row = jnp.zeros((1, C), f32)
    for h in range(HL):
        same_row = jnp.where(lane_head == h, vbias[0, head * HL + h], same_row)
        other_row = jnp.where(lane_head == h, vbias[1, head * HL + h], other_row)

    def split(row):
        one = row.astype(bf16).astype(f32)
        two = (row - one).astype(bf16).astype(f32)
        three = (row - one - two).astype(bf16).astype(f32)
        term = iota((BROWS, C), 0) // NVAR
        return jnp.where(term == 0, one, jnp.where(term == 1, two, jnp.where(term == 2, three, 0.0)))

    same_terms = split(same_row)
    other_terms = split(other_row)
    brow = iota((BROWS, C), 0)
    trow = iota((BROWS, tree), 0)
    for r in range(R):
        line = tvar[:, r * tree : (r + 1) * tree]
        hot = jnp.where(trow < TERMS * NVAR, (line == trow % NVAR).astype(f32), 0.0).astype(bf16)
        tvoh[r] = hot
        matched = dot(hot, spread) > 0.5
        terms = jnp.where(matched, same_terms, other_terms)
        bmat[r] = jnp.where(brow == TERMS * NVAR, low, terms).astype(bf16)

    up = parents[...]
    eye = (iota((tree, tree), 0) == iota((tree, tree), 1)).astype(f32)
    reach = ((iota((tree, tree), 0) == up).astype(f32) + eye).astype(bf16)
    clip = lambda v: jnp.minimum(v, 1.0).astype(bf16)
    reach2 = clip(dot(reach, reach))
    reach4 = clip(dot(reach2, reach2))
    reach8 = clip(dot(reach4, reach4))
    allowed = dot(reach8, spread) > 0.5

    def spread_query(q):
        return jnp.concatenate([q] * HL, axis=0) * block

    tree_scores = dot(keys, spread_query(query)) + dot(tvoh[req], bmat[req], 0, 0)
    tree_max = jnp.max(jnp.where(allowed, tree_scores, low), axis=0, keepdims=True)
    tree_w = jnp.where(allowed, jnp.exp(tree_scores - tree_max), 0.0).astype(bf16)
    tree_total = jnp.sum(tree_w.astype(f32), axis=0, keepdims=True)
    tree_out = pick(dot(vals, tree_w, 0, 0))

    get_pages.wait()

    @pl.loop(0, pool // group)
    def _(g):
        for k in range(group):
            vt[g * group + k] = pages[1, g * group + k].T
            oht[g * group + k] = oh[g * group + k].T

    @pl.loop(0, half)
    def _(k):
        forward_copy(k).wait()

    wide = 10 if pool % 10 == 0 else 1

    @pl.loop(0, pool // wide)
    def _(g):
        for k in range(wide):
            p = g * wide + k
            owner = own_s[p]
            scores = dot(pages[0, p], spread_query(qbuf[owner])) + dot(oht[p], bmat[owner])
            top = jnp.max(scores, axis=0, keepdims=True)
            w = jnp.exp(scores - top).astype(bf16)
            pm[pl.ds(p, 1), :] = top
            plt[pl.ds(p, 1), :] = jnp.sum(w.astype(f32), axis=0, keepdims=True)
            po[p] = pick(dot(vt[p], w))

    def out_copy(d):
        return remote(osend.at[d], obuf.at[d], os_.at[d], or_.at[d], at_req(d))

    def stat_copy(d):
        return remote(ssend.at[d], sbuf.at[d], ss.at[d], sr.at[d], at_req(d))

    def merged(r):
        mask = own_rows[...] == r
        maxes = pm[...]
        top = jnp.max(jnp.where(mask, maxes, low), axis=0, keepdims=True)
        factor = jnp.where(mask, jnp.exp(maxes - top), 0.0)
        total = jnp.sum(factor * plt[...], axis=0, keepdims=True)
        out = factor[0:1] * po[0]
        for p in range(1, pool):
            out = out + factor[p : p + 1] * po[p]
        return top, total, out

    @pl.loop(1, R)
    def _(d):
        top, total, out = merged(lax.rem(req + d, R))
        osend[d] = out.astype(bf16)
        ssend[d] = jnp.concatenate([top, total], axis=0)
        out_copy(d).start()
        stat_copy(d).start()

    top, total, out = merged(req)
    new_top = jnp.maximum(top, tree_max)
    fa = jnp.exp(top - new_top)
    fb = jnp.exp(tree_max - new_top)
    total = total * fa + tree_total * fb
    out = out * fa + tree_out * fb
    top = new_top

    @pl.loop(1, R)
    def _(d):
        out_copy(d).wait()
        stat_copy(d).wait()

    final_top = top
    for d in range(1, R):
        final_top = jnp.maximum(final_top, sbuf[d][0:1])
    fa = jnp.exp(top - final_top)
    total = total * fa
    out = out * fa
    for d in range(1, R):
        stats = sbuf[d]
        fd = jnp.exp(stats[0:1] - final_top)
        total = total + stats[1:2] * fd
        out = out + obuf[d].astype(f32) * fd
    att_t = (out / total).astype(bf16)
    att = dot(spread, spread_query(att_t), 1, 1).astype(bf16)
    gbuf[head] = att
    att_copies = [remote(gbuf.at[head], gbuf.at[head], gs.at[d - 1], gr.at[d - 1], at_head(d)) for d in range(1, H)]
    for copy in att_copies:
        copy.start()
    attended[...] = att
    get_out.wait()
    state = values + dot(att, outw[pl.ds(pl.multiple_of(head * QL, QL), QL), :])
    for d in range(1, H):
        att_copies[d - 1].wait()
        source = lax.rem(head + H - d, H)
        state = state + dot(gbuf[source], outw[pl.ds(pl.multiple_of(source * QL, QL), QL), :])
    state = state.astype(bf16).astype(f32)
    hid[...] = state.reshape(H, rows, D)
    normed_two = rms_scaled(state, gains[1:2, :]).astype(bf16)
    get_gu.wait()
    step = STEP
    for c in range(0, FFL, step):
        gate = dot(normed_two, gu[0, :, c : c + step])
        upward = dot(normed_two, gu[1, :, c : c + step])
        act[:, c : c + step] = (gate / (1.0 + jnp.exp(-gate)) * upward).astype(bf16)
    get_down.wait()
    activated = act[...]
    def down_copy(d, n):
        columns = pl.ds(n * step, step)
        return remote(
            dsend.at[lax.rem(head + d, H), :, columns], dbuf.at[d - 1, :, columns],
            ds_.at[d - 1, n], dr.at[d - 1, n], at_head(d),
        )

    for n in range(D // step):
        part = dot(activated, downw[:, n * step : (n + 1) * step])
        dsend[:, :, n * step : (n + 1) * step] = part.reshape(H, rows, step).astype(bf16)
        for d in range(1, H):
            down_copy(d, n).start()
    result = dsend[head].astype(f32)
    for d in range(1, H):
        for n in range(D // step):
            down_copy(d, n).wait()
        result = result + dbuf[d - 1].astype(f32)
    mixed[...] = (hid[head] + result).astype(bf16)


def hand_over(mixed, attended, new_kv, mixed_out, attended_out, new_kv_out, one, two, three, sem):
    fetch = [
        pltpu.make_async_copy(src, dst, sem.at[k])
        for k, (src, dst) in enumerate(((mixed, one), (attended, two), (new_kv, three)))
    ]
    store = [
        pltpu.make_async_copy(src, dst, sem.at[3 + k])
        for k, (src, dst) in enumerate(((one, mixed_out), (two, attended_out), (three, new_kv_out)))
    ]
    for copy in fetch:
        copy.start()
    for k in range(3):
        fetch[k].wait()
        store[k].start()
    for copy in store:
        copy.wait()


def shards(
    tokens, gains, qkv_weight, out_weight, gate_up_weight, down_weight, variate_bias, page_cache, page_variates,
    token_variates, cache_len, page_table, parents, accepted,
):
    R = lax.axis_size("req")
    H = lax.axis_size("head")
    rows, D = tokens.shape
    QL = qkv_weight.shape[2]
    HL = QL // HD
    pool, page = page_variates.shape
    tree = parents.shape[1]
    C = HL * tree
    padded = (pool + 7) // 8 * 8
    hbm = pl.BlockSpec(memory_space=pl.ANY)
    vmem = pl.BlockSpec(memory_space=pltpu.VMEM)
    dma = pltpu.SemaphoreType.DMA
    results = pl.pallas_call(
        functools.partial(kernel, R, H),
        out_shape=(
            jax.ShapeDtypeStruct((rows, D), bf16),
            jax.ShapeDtypeStruct((tree, QL), bf16),
            jax.ShapeDtypeStruct((2, 1, accepted.shape[1], QL), bf16),
        ),
        in_specs=[hbm] * 14,
        out_specs=(vmem, vmem, vmem),
        scratch_shapes=[
            pltpu.VMEM(gains.shape, f32),
            pltpu.SMEM(variate_bias.shape, f32),
            pltpu.VMEM(page_variates.shape, jnp.int32),
            pltpu.VMEM((1, token_variates.shape[0]), jnp.int32),
            pltpu.SMEM(cache_len.shape, jnp.int32),
            pltpu.VMEM(page_table.shape, jnp.int32),
            pltpu.VMEM(parents.shape, jnp.int32),
            pltpu.VMEM(accepted.shape, jnp.int32),
            pltpu.VMEM((pool, QL, page), bf16),
            pltpu.VMEM((pool, page, BROWS), bf16),
            pltpu.VMEM(qkv_weight.shape, bf16),
            pltpu.VMEM(out_weight.shape, bf16),
            pltpu.VMEM(gate_up_weight.shape, bf16),
            pltpu.VMEM(down_weight.shape, bf16),
            pltpu.VMEM(page_cache.shape, bf16),
            pltpu.VMEM((H, rows, D), bf16),
            pltpu.VMEM((R, HD, C), bf16),
            pltpu.VMEM((R, BROWS, tree), bf16),
            pltpu.VMEM((R, BROWS, C), bf16),
            pltpu.VMEM((pool, BROWS, page), bf16),
            pltpu.SMEM((pool,), jnp.int32),
            pltpu.VMEM((padded, C), jnp.int32),
            pltpu.VMEM((padded, C), f32),
            pltpu.VMEM((padded, C), f32),
            pltpu.VMEM((pool, HD, C), f32),
            pltpu.VMEM((R, HD, C), bf16),
            pltpu.VMEM((R, 2, C), f32),
            pltpu.VMEM((R, HD, C), bf16),
            pltpu.VMEM((R, 2, C), f32),
            pltpu.VMEM((H, tree, QL), bf16),
            pltpu.VMEM((tree, gate_up_weight.shape[2]), bf16),
            pltpu.VMEM((H, rows, D), f32),
            pltpu.VMEM((H, rows, D), bf16),
            pltpu.VMEM((H, rows, D), bf16),
            dma((6,)),
            dma((8,)),
            dma((H,)), dma((H,)),
            dma((R,)), dma((R,)),
            dma((R,)), dma((R,)),
            dma((R,)), dma((R,)),
            dma((R,)), dma((R,)),
            dma((H,)), dma((H,)),
            dma((H, D // STEP)), dma((H, D // STEP)),
        ],
        compiler_params=pltpu.CompilerParams(
            collective_id=0, has_side_effects=True, vmem_limit_bytes=60 * 1024 * 1024
        ),
        cost_estimate=pl.CostEstimate(flops=10**9, bytes_accessed=12 * 10**6, transcendentals=10**6),
    )(
        tokens, gains, qkv_weight, out_weight, gate_up_weight, down_weight, variate_bias, page_cache, page_variates,
        token_variates.reshape(1, -1), cache_len, page_table, parents, accepted,
    )
    return tuple(pl.pallas_call(
        hand_over,
        out_shape=tuple(jax.ShapeDtypeStruct(a.shape, a.dtype) for a in results),
        in_specs=[hbm] * 3,
        out_specs=(hbm,) * 3,
        scratch_shapes=[pltpu.VMEM(a.shape, a.dtype) for a in results] + [dma((6,))],
        compiler_params=pltpu.CompilerParams(vmem_limit_bytes=60 * 1024 * 1024),
    )(*results))


def solution(mesh):
    return jax.shard_map(
        shards,
        mesh=mesh,
        in_specs=(
            P(("req", "head"), None),
            P(),
            P(None, None, "head"),
            P(),
            P(None, None, "head"),
            P("head", None),
            P(),
            P(None, "req", None, "head"),
            P("req", None),
            P(),
            P(),
            P(),
            P("req", None),
            P("req", None),
        ),
        out_specs=(P(("req", "head"), None), P("req", "head"), P(None, "req", None, "head")),
        check_vma=False,
    )
```
